32 devices in a mesh: noise: 2 (over y), patch: 16 (over z, x, core).
Axes of the slice: x: 2, y: 2, z: 4, core: 2. Of those that a mesh axis runs over, the one named last changes fastest.
Arguments:
- nodes: bfloat16 [2, 8192, 512], P('noise', 'patch'), may hold values from -6 to 6
- noise_level: float32 [2], P('noise'), may hold values from 0.03 to 80
- patch_sizes: int32 [16], P('patch'), may hold values from 256 to 512, as said below
- send_rows: int32 [2048], P('patch'), may hold values from 0 to 511, as said below
- neighbours: int32 [16, 8192], P(None, 'patch'), may hold values from 0 to 639, as said below
- qkv_weight: bfloat16 [2, 512, 1536], replicated, may hold values from -0.25 to 0.25
- out_weight: bfloat16 [2, 512, 512], replicated, may hold values from -0.5 to 0.5
- up_weight: bfloat16 [2, 512, 2048], replicated, may hold values from -0.25 to 0.25
- down_weight: bfloat16 [2, 2048, 512], replicated, may hold values from -0.125 to 0.125
- cond_weight: bfloat16 [2, 4, 32, 512], replicated, may hold values from -0.5 to 0.5
- cotangent: bfloat16 [2, 8192, 512], P('noise', 'patch'), may hold values from -6 to 6
Outputs:
- result: bfloat16 [2, 8192, 512], P('noise', 'patch')
- input_grad: float32 [2, 8192, 512], P('noise', 'patch')
- qkv_grad: float32 [2, 512, 1536], replicated
- out_grad: float32 [2, 512, 512], replicated
- up_grad: float32 [2, 512, 2048], replicated
- down_grad: float32 [2, 2048, 512], replicated
- cond_grad: float32 [2, 4, 32, 512], replicated
The draws below stay inside these ranges and needn't reach their ends.
Inputs may be any that keep to these rules, and one draw needn't show every extreme that they name: `patch_sizes`: live rows of each patch, between half of 512 and 512; one patch has exactly 512, another exactly 256. `send_rows`: block p (128 entries) holds rows of patch p below its size; its first 64 go to the patch before, its last 64 to the patch after, the patches forming a loop. `neighbours`: an entry below 512 is a row of the node's own patch, from 512 to 575 one received from the patch before, above it one received from the patch after; a live node names only live rows of its patch or received rows; entry 0 is the node itself.
All inputs are finite; a program needn't handle non-finite values.
Results may differ from the reference program's by a relative error of at most 0.018.
Values may be sent and summed in bfloat16 or wider, within the bound.
A program may use at most 256 MiB of HBM per device.

```python
import math
import jax
import jax.numpy as jnp
from jax import lax

D = 512
HEADS = 4
HEAD = 128
FF = 2048
K = 16
COND = 32
LAYERS = 2
CAP = 512
SEND = 64
NODES = 8192
LEVELS = 2
N_PATCH = 16


def sizes_common(key):
    key = jax.random.fold_in(key, 101)
    key_base, key_first, key_second = jax.random.split(key, 3)
    drawn_sizes = jax.random.randint(key_base, (N_PATCH,), CAP // 2, CAP + 1)
    first_patch = jax.random.randint(key_first, (), 0, N_PATCH)
    second_patch = (first_patch + 1 + jax.random.randint(key_second, (), 0, N_PATCH - 1)) % N_PATCH
    places = jnp.arange(N_PATCH)
    drawn_sizes = jnp.where(places == first_patch, CAP, drawn_sizes)
    drawn_sizes = jnp.where(places == second_patch, CAP // 2, drawn_sizes)
    return drawn_sizes.astype(jnp.int32)


def draw_patch_sizes(key, part):
    return sizes_common(key)


def draw_send_rows(key, part):
    patch_rows = sizes_common(key)
    key = jax.random.fold_in(key, 2)
    picks = jax.random.randint(key, (N_PATCH, 2 * SEND), 0, 1 << 20)
    chosen = picks % patch_rows[:, None]
    column_id = jnp.arange(2 * SEND)[None, :]
    chosen = jnp.where(column_id == 0, patch_rows[:, None] - 1, chosen)
    chosen = jnp.where(column_id == 2 * SEND - 1, 0 * chosen, chosen)
    return chosen.reshape(N_PATCH * 2 * SEND).astype(jnp.int32)


def draw_neighbours(key, part):
    patch_rows = sizes_common(key)
    key = jax.random.fold_in(key, 3)
    key_local, key_remote, key_which = jax.random.split(key, 3)
    grid_shape = (N_PATCH, CAP, K)
    local_rows = jax.random.randint(key_local, grid_shape, 0, 1 << 20) % patch_rows[:, None, None]
    remote_rows = CAP + jax.random.randint(key_remote, grid_shape, 0, 2 * SEND)
    which_one = jax.random.randint(key_which, grid_shape, 0, 2)
    slot_id = jnp.arange(K)[None, None, :]
    row_id = jnp.arange(CAP)[None, :, None]
    chosen = jnp.where((slot_id >= K - 4) & (which_one == 1), remote_rows, local_rows)
    chosen = jnp.where(slot_id == 0, row_id + 0 * chosen, chosen)
    chosen = jnp.where((row_id == 0) & (slot_id == K - 1), CAP + 2 * SEND - 1, chosen)
    return chosen.reshape(NODES, K).T.astype(jnp.int32)


def block_levels(rng, extent, cuts, smallest, high):
    def one(position, shards_of):
        steps = jax.random.uniform(jax.random.fold_in(jax.random.fold_in(rng, 6), position), (shards_of,), jnp.float32, smallest / len(cuts), high / len(cuts))
        return jnp.repeat(jnp.exp(steps), extent[position] // shards_of).reshape((-1,) + (1,) * (len(extent) - position - 1))

    factor_of = one(*cuts[0])
    for cut in cuts[1:]:
        factor_of = factor_of * one(*cut)
    return factor_of


def gaussian(key, shape, spread, bound, pieces=(), kind=jnp.bfloat16):
    values = spread * jax.random.normal(key, shape, jnp.float32)
    if pieces:
        values = values * block_levels(key, shape, pieces, -0.22, 0.18)
    return jnp.clip(values, -bound, bound).astype(kind)


def setup_inputs(seed: int = 0) -> dict:
    seeds = jax.random.split(jax.random.key(seed), 12)
    return {
        "nodes": gaussian(seeds[0], (LEVELS, NODES, D), 1.0, 6.0, ((0, 2), (1, 16))),
        "noise_level": jnp.clip(jnp.exp(math.log(80.0) - 7.8885846 * jax.random.uniform(seeds[1], (LEVELS,), jnp.float32) ** block_levels(seeds[1], (LEVELS,), ((0, 2),), -0.2, 0.2)), 0.03, 80.0),
        "patch_sizes": draw_patch_sizes(jax.random.fold_in(seeds[11], 71), 0),
        "send_rows": draw_send_rows(jax.random.fold_in(seeds[11], 71), 0),
        "neighbours": draw_neighbours(jax.random.fold_in(seeds[11], 71), 0),
        "qkv_weight": gaussian(seeds[5], (LAYERS, D, 3 * D), D ** -0.5, 0.25),
        "out_weight": gaussian(seeds[6], (LAYERS, D, D), (D // 4) ** -0.5, 0.5),
        "up_weight": gaussian(seeds[7], (LAYERS, D, FF), D ** -0.5, 0.25),
        "down_weight": gaussian(seeds[8], (LAYERS, FF, D), FF ** -0.5, 0.125),
        "cond_weight": gaussian(seeds[9], (LAYERS, 4, COND, D), (4 * COND) ** -0.5, 0.5),
        "cotangent": gaussian(seeds[10], (LEVELS, NODES, D), 1.0, 6.0, ((0, 2), (1, 16))),
    }


EPSILON = 1e-05
HIGHEST = lax.Precision.HIGHEST

@jax.custom_vjp
def low(v):
    return lax.optimization_barrier(v.astype(jnp.bfloat16)).astype(jnp.float32)

@jax.custom_vjp
def low_back(v):
    return v

def low_keep(v):
    return (low(v), None)

def low_pass(kept, grad):
    return (grad,)

def back_keep(v):
    return (v, None)

def back_low(kept, grad):
    return (low(grad),)
low.defvjp(low_keep, low_pass)
low_back.defvjp(back_keep, back_low)

def product(left, right):
    return jnp.dot(left, right, precision=HIGHEST, preferred_element_type=jnp.float32)

def features(noise):
    frequency = 2.0 ** (jnp.arange(COND // 2, dtype=jnp.float32) / 4.0)
    phase_arg = jnp.log(noise) * frequency
    return jnp.concatenate([jnp.sin(phase_arg), jnp.cos(phase_arg)])

def layer_norm(hidden):
    row_mean = lax.optimization_barrier(jnp.mean(hidden, -1, keepdims=True))
    centred = hidden - row_mean
    return centred * lax.rsqrt(lax.optimization_barrier(jnp.mean(centred * centred, -1, keepdims=True)) + EPSILON)

def source_rows(neighbours, send_rows):
    entries = neighbours.T
    sent = send_rows.reshape(N_PATCH, 2 * SEND)
    patch_id = (jnp.arange(NODES, dtype=jnp.int32) // CAP)[:, None]
    left_patch = (patch_id - 1) % N_PATCH
    right_patch = (patch_id + 1) % N_PATCH
    from_left = sent[left_patch, jnp.clip(entries - CAP + SEND, 0, 2 * SEND - 1)]
    from_right = sent[right_patch, jnp.clip(entries - CAP - SEND, 0, 2 * SEND - 1)]
    remote = jnp.where(entries < CAP + SEND, left_patch * CAP + from_left, right_patch * CAP + from_right)
    return jnp.where(entries < CAP, patch_id * CAP + entries, remote).astype(jnp.int32)

def attend(query, kv_rows, source):
    block_rows = min(512, CAP)
    block_count = NODES // block_rows

    def one_block(inputs):
        query_block, index_block = inputs
        gathered = kv_rows[index_block].reshape(block_rows, K, 2, HEADS, HEAD)
        query_heads = query_block.reshape(block_rows, HEADS, HEAD)
        scores = jnp.einsum('nhd,njhd->njh', query_heads, gathered[:, :, 0], precision=HIGHEST) * HEAD ** (-0.5)
        scores = low_back(scores)
        highest = lax.optimization_barrier(jnp.max(scores, 1, keepdims=True))
        exponent = jnp.exp(scores - highest)
        attn_prob = low(exponent / lax.optimization_barrier(jnp.sum(exponent, 1, keepdims=True)))
        attended = jnp.einsum('njh,njhd->nhd', attn_prob, gathered[:, :, 1], precision=HIGHEST)
        return attended.reshape(block_rows, D)
    result_blocks = lax.map(jax.checkpoint(one_block), (query.reshape(block_count, block_rows, D), source.reshape(block_count, block_rows, K)))
    return result_blocks.reshape(NODES, D)

def residual_layer(hidden, cond_rows, qkv_in, out_in, up_in, down_in, source):
    first_input = low(layer_norm(hidden) * (1.0 + cond_rows[0]) + cond_rows[1])
    projected = product(first_input, qkv_in)
    query = low_back(low(projected[:, :D]))
    kv_rows = low_back(low(projected[:, D:]))
    attended = low_back(low(attend(query, kv_rows, source)))
    middle = hidden + low_back(product(attended, out_in))
    second_input = low(layer_norm(middle) * (1.0 + cond_rows[2]) + cond_rows[3])
    pre_act = low_back(product(second_input, up_in))
    activation = low(pre_act * jax.nn.sigmoid(pre_act))
    return middle + low_back(product(activation, down_in))

def reference(nodes, noise_level, patch_sizes, send_rows, neighbours, qkv_weight, out_weight, up_weight, down_weight, cond_weight, cotangent):
    source = source_rows(neighbours, send_rows)
    node_ids = jnp.arange(NODES, dtype=jnp.int32)
    live_mask = (node_ids % CAP < patch_sizes[node_ids // CAP]).astype(jnp.float32)[:, None]

    def forward(node_in, qkv_in, out_in, up_in, down_in, cond_in):
        results = []
        for level_id in range(LEVELS):
            noise_feats = features(noise_level[level_id])
            hidden = node_in[level_id]
            for layer_id in range(LAYERS):
                cond_rows = jnp.einsum('c,icd->id', noise_feats, cond_in[layer_id], precision=HIGHEST)
                hidden = residual_layer(hidden, cond_rows, qkv_in[layer_id], out_in[layer_id], up_in[layer_id], down_in[layer_id], source)
            results.append(hidden * live_mask)
        return jnp.stack(results)
    primals = tuple((entry.astype(jnp.float32) for entry in (nodes, qkv_weight, out_weight, up_weight, down_weight, cond_weight)))
    output, pullback = jax.vjp(forward, *primals)
    gradients = pullback(cotangent.astype(jnp.float32))
    return (output.astype(jnp.bfloat16), gradients[0], gradients[1], gradients[2], gradients[3], gradients[4], gradients[5])
```

```python
import functools

import jax
import jax.numpy as jnp
import numpy as np
from jax import lax
from jax.experimental import pallas as pl
from jax.experimental.pallas import tpu as pltpu
from jax.sharding import PartitionSpec as P

HEADS = 4
COND = 32
EPSILON = 1e-05
LOG2E = 1.4426950408889634
MESH = pl.DeviceIdType.MESH
F32 = jnp.float32
BF16 = jnp.bfloat16
BLOCK = 512


def nn(a, b):
    return lax.dot_general(a, b, (((1,), (0,)), ((), ())), preferred_element_type=F32)


def nt(a, b):
    return lax.dot_general(a, b, (((1,), (1,)), ((), ())), preferred_element_type=F32)


def tn(a, b):
    return lax.dot_general(a, b, (((0,), (0,)), ((), ())), preferred_element_type=F32)


def mega(
    patches,
    noise_ref,
    sizes_ref,
    send_ref,
    nbr_ref,
    cond_w_ref,
    freq_ref,
    nodes_hbm,
    qkv_hbm,
    out_hbm,
    up_hbm,
    down_hbm,
    cot_hbm,
    result_ref,
    igrad_ref,
    grad_hbm,
    sums_ref,
    w,
    logc,
    sel,
    sel_t,
    cond,
    hid,
    mid,
    xh1,
    xh2,
    rs1,
    rs2,
    act1,
    act2,
    low,
    tr,
    qv,
    kv,
    prob,
    att_t,
    gate,
    slope,
    dob,
    dkv,
    dqkv,
    rim,
    rin,
    node_in,
    cot_in,
    load_sem,
    halo_send,
    halo_recv,
    out_sem,
):
    rows = hid.shape[0]
    table = kv.shape[1]
    halo = rim.shape[0] // 2
    my_noise = lax.axis_index("noise")
    me = lax.axis_index("patch")
    before = (my_noise, lax.rem(me + patches - 1, patches))
    after = (my_noise, lax.rem(me + 1, patches))

    def source(t, k):
        if k < 4:
            return down_hbm.at[t, pl.ds(k * BLOCK, BLOCK), :]
        if k < 8:
            return up_hbm.at[t, :, pl.ds((k - 4) * BLOCK, BLOCK)]
        if k < 9:
            return out_hbm.at[t]
        return qkv_hbm.at[t, :, pl.ds((k - 9) * BLOCK, BLOCK)]

    def load(t, k):
        return pltpu.make_async_copy(source(t, k), w.at[(1 - t) * 12 + k], load_sem.at[t, k])

    node_copy = pltpu.make_async_copy(nodes_hbm.at[0], node_in, load_sem.at[2, 0])
    cot_copy = pltpu.make_async_copy(cot_hbm.at[0], cot_in, load_sem.at[2, 1])
    node_copy.start()
    for t in range(2):
        for k in (9, 10, 11, 8, 4, 0, 5, 1, 6, 2, 7, 3):
            load(t, k).start()
    cot_copy.start()

    barrier = pltpu.get_barrier_semaphore()
    for other in (before, after):
        pl.semaphore_signal(barrier, inc=1, device_id=other, device_id_type=MESH)

    step_rows = 64

    def count(i, _):
        base = i * step_rows
        ids = lax.broadcasted_iota(jnp.int32, (step_rows, rows), 0) + base
        total = jnp.zeros((step_rows, rows), F32)
        for j in range(nbr_ref.shape[0]):
            total = total + jnp.where(nbr_ref[j : j + 1, :] == ids, 1.0, 0.0)
        logc[pl.ds(base, step_rows), :] = jnp.where(total > 0.0, jnp.log(total) * LOG2E, -1e30)
        return 0

    lax.fori_loop(0, table // step_rows, count, 0)
    picked = jnp.where(
        lax.broadcasted_iota(jnp.int32, (rows, 2 * halo), 0) == send_ref[...], 1.0, 0.0
    )
    sel_t[...] = picked.astype(BF16)
    sel[...] = picked.T.astype(BF16)

    phase = jnp.log(jnp.full((COND, 128), noise_ref[0], F32)) * freq_ref[...]
    is_sin = lax.broadcasted_iota(jnp.int32, (COND, 128), 0) < COND // 2
    feats = jnp.where(is_sin, jnp.sin(phase), jnp.cos(phase))
    wide = jnp.concatenate([feats] * (hid.shape[1] // 128), axis=1)
    for t in range(2):
        for i in range(4):
            cond[t * 4 + i] = jnp.sum(cond_w_ref[t, i].astype(F32) * wide, 0, keepdims=True)

    node_copy.wait()
    hid[...] = node_in[...].astype(F32)
    pl.semaphore_wait(barrier, 2)

    head = hid.shape[1] // HEADS
    unit = LOG2E * head ** (-0.5)
    ln_rows = 64

    def norm(value_ref, t, first, normed_ref, inv_ref, out_ref):
        def body(i, _):
            at = pl.ds(i * ln_rows, ln_rows)
            value = value_ref[at, :]
            centred = value - jnp.mean(value, -1, keepdims=True)
            inv = lax.rsqrt(jnp.mean(centred * centred, -1, keepdims=True) + EPSILON)
            normed = centred * inv
            normed_ref[t, at, :] = normed
            inv_ref[t, at, :] = inv
            out_ref[t, at, :] = (
                normed * (1.0 + cond[t * 4 + first]) + cond[t * 4 + first + 1]
            ).astype(BF16)
            return 0

        lax.fori_loop(0, rows // ln_rows, body, 0)

    def halo_copies(stage, src, dst_before, dst_after):
        return [
            pltpu.make_async_remote_copy(
                src_ref=src.at[pl.ds(0, halo)],
                dst_ref=dst_before,
                send_sem=halo_send.at[stage, 0],
                recv_sem=halo_recv.at[stage, 0],
                device_id=before,
                device_id_type=MESH,
            ),
            pltpu.make_async_remote_copy(
                src_ref=src.at[pl.ds(halo, halo)],
                dst_ref=dst_after,
                send_sem=halo_send.at[stage, 1],
                recv_sem=halo_recv.at[stage, 1],
                device_id=after,
                device_id_type=MESH,
            ),
        ]

    def forward(t, _):
        base = (1 - t) * 12
        for k in range(12):
            load_wait(t, k)
        norm(hid, t, 0, xh1, rs1, act1)
        a = act1[t]
        kv[t, pl.ds(0, rows), pl.ds(0, BLOCK)] = nn(a, w[base + 10]).astype(BF16)
        kv[t, pl.ds(0, rows), pl.ds(BLOCK, BLOCK)] = nn(a, w[base + 11]).astype(BF16)
        rim[...] = nn(sel[...], kv[t, pl.ds(0, rows), :]).astype(BF16)
        copies = halo_copies(
            t, rim, kv.at[t, pl.ds(rows + halo, halo), :], kv.at[t, pl.ds(rows, halo), :]
        )
        for copy in copies:
            copy.start()
        qv[t] = nn(a, w[base + 9]).astype(BF16)
        for copy in copies:
            copy.wait()
        for h in range(HEADS):
            keys = kv[t, :, pl.ds(h * head, head)]
            values = kv[t, :, pl.ds(BLOCK + h * head, head)]
            for c in range(2):
                cols = pl.ds(c * 256, 256)
                score = nt(keys, qv[t, cols, pl.ds(h * head, head)]) * unit + logc[:, cols]
                part = jnp.exp2(score - jnp.max(score, 0, keepdims=True))
                weight = (part * (1.0 / jnp.sum(part, 0, keepdims=True))).astype(BF16)
                prob[t, h, :, cols] = weight
                att_t[t, pl.ds(h * head, head), cols] = tn(values, weight).astype(BF16)
        mid[...] = hid[...] + tn(att_t[t], w[base + 8])
        norm(mid, t, 2, xh2, rs2, act2)
        for f in range(4):
            u = nn(act2[t], w[base + 4 + f])
            sig = 0.5 * jnp.tanh(0.5 * u) + 0.5
            g = u * sig
            gate[t, f] = g.astype(BF16)
            slope[t, f] = (sig + g * (1.0 - sig)).astype(BF16)
            if f == 0:
                hid[...] = mid[...] + nn(gate[t, f], w[base + f])
            else:
                hid[...] += nn(gate[t, f], w[base + f])
        return 0

    def load_wait(t, k):
        pltpu.make_async_copy(
            out_hbm.at[0], w.at[(1 - t) * 12 + k], load_sem.at[t, k]
        ).wait()

    lax.fori_loop(0, 2, forward, 0)

    cot_copy.wait()

    def turn(i, _):
        at = pl.ds(i * ln_rows, ln_rows)
        ids = lax.broadcasted_iota(jnp.int32, (ln_rows, hid.shape[1]), 0) + i * ln_rows
        live = ids < sizes_ref[0]
        result_ref[0, at, :] = jnp.where(live, hid[at, :], 0.0).astype(BF16)
        hid[at, :] = jnp.where(live, cot_in[at, :].astype(F32), 0.0)
        return 0

    lax.fori_loop(0, rows // ln_rows, turn, 0)

    def norm_back(t, first, grad_ref, normed_ref, inv_ref, add_ref, out_ref):
        def body(i, carry):
            scale_sum, shift_sum = carry
            at = pl.ds(i * ln_rows, ln_rows)
            grad = grad_ref[at, :]
            normed = normed_ref[t, at, :]
            back = grad * normed
            scale_sum = scale_sum + jnp.sum(back, 0, keepdims=True)
            shift_sum = shift_sum + jnp.sum(grad, 0, keepdims=True)
            scaled = grad * (1.0 + cond[t * 4 + first])
            one = jnp.mean(scaled, -1, keepdims=True)
            two = jnp.mean(scaled * normed, -1, keepdims=True)
            out = add_ref[at, :] + inv_ref[t, at, :] * (scaled - one - normed * two)
            out_ref[at, :] = out
            low[at, :] = out.astype(BF16)
            return scale_sum, shift_sum

        zero = jnp.zeros((1, hid.shape[1]), F32)
        scale_sum, shift_sum = lax.fori_loop(0, rows // ln_rows, body, (zero, zero))
        sums_ref[t * 4 + first] = scale_sum
        sums_ref[t * 4 + first + 1] = shift_sum

    low[...] = hid[...].astype(BF16)

    def backward(i, _):
        t = 1 - i
        base = i * 12
        for f in range(4):
            slope[t, f] = (nt(low[...], w[base + f]) * slope[t, f].astype(F32)).astype(BF16)
        for f in range(4):
            w[base + f] = tn(gate[t, f], low[...]).astype(BF16)
        for f in range(4):
            if f == 0:
                mid[...] = nt(slope[t, f], w[base + 4 + f])
            else:
                mid[...] += nt(slope[t, f], w[base + 4 + f])
        tr[...] = act2[t].T
        for f in range(4):
            w[base + 4 + f] = nn(tr[...], slope[t, f]).astype(BF16)
        norm_back(t, 2, mid, xh2, rs2, hid, mid)
        dob[...] = nt(low[...], w[base + 8]).astype(BF16)
        w[base + 8] = nn(att_t[t], low[...]).astype(BF16)
        for h in range(HEADS):
            lanes = pl.ds(h * head, head)
            keys = kv[t, :, lanes]
            values = kv[t, :, pl.ds(BLOCK + h * head, head)]
            weight = prob[t, h]
            grad_out = dob[:, lanes]
            grad_weight = nt(values, grad_out)
            spread = weight.astype(F32) * grad_weight
            delta = jnp.sum(spread, 0, keepdims=True)
            ds = (spread - weight.astype(F32) * delta).astype(BF16)
            dv = nn(weight, grad_out)
            dk = nn(ds, qv[t, :, lanes]) * (head ** (-0.5))
            dq_t = tn(keys, ds) * (head ** (-0.5))
            dqkv[:, lanes] = dq_t.T.astype(BF16)
            dkv[:, lanes] = dk[:rows]
            dkv[:, pl.ds(BLOCK + h * head, head)] = dv[:rows]
            rim[:, lanes] = dk[rows:].astype(BF16)
            rim[:, pl.ds(BLOCK + h * head, head)] = dv[rows:].astype(BF16)
        copies = halo_copies(
            2 + t, rim, rin.at[t, pl.ds(halo, halo), :], rin.at[t, pl.ds(0, halo), :]
        )
        for copy in copies:
            copy.start()
        tr[...] = act1[t].T
        dob[...] = nn(tr[...], dqkv[:, pl.ds(0, BLOCK)]).astype(BF16)
        for copy in copies:
            copy.wait()
        dqkv[:, pl.ds(BLOCK, 2 * BLOCK)] = (dkv[...] + nn(sel_t[...], rin[t])).astype(BF16)
        back = nt(dqkv[:, pl.ds(0, BLOCK)], w[base + 9])
        for k in range(1, 3):
            back = back + nt(dqkv[:, pl.ds(k * BLOCK, BLOCK)], w[base + 9 + k])
        hid[...] = back
        w[base + 9] = dob[...]
        for k in range(1, 3):
            w[base + 9 + k] = nn(tr[...], dqkv[:, pl.ds(k * BLOCK, BLOCK)]).astype(BF16)
        norm_back(t, 0, hid, xh1, rs1, mid, hid)
        return 0

    lax.fori_loop(0, 2, backward, 0)
    igrad_ref[0] = hid[...]
    out_copy = pltpu.make_async_copy(w, grad_hbm, out_sem)
    out_copy.start()
    out_copy.wait()


def solution(mesh):
    patches = mesh.shape["patch"]

    def shards(nodes, noise, sizes, send, nbr, qkv, out, up, down, cond_w, cot):
        rows, width = nodes.shape[1:]
        halo2 = send.shape[0]
        halo = halo2 // 2
        table = rows + halo2
        freq = np.tile(2.0 ** (np.arange(COND) % (COND // 2) / 4.0), (128, 1)).T.astype(np.float32)
        vmem = pl.BlockSpec(memory_space=pltpu.VMEM)
        smem = pl.BlockSpec(memory_space=pltpu.SMEM)
        hbm = pl.BlockSpec(memory_space=pl.ANY)
        result, igrad, grads, sums = pl.pallas_call(
            functools.partial(mega, patches),
            out_shape=(
                jax.ShapeDtypeStruct((1, rows, width), BF16),
                jax.ShapeDtypeStruct((1, rows, width), F32),
                jax.ShapeDtypeStruct((24, BLOCK, BLOCK), BF16),
                jax.ShapeDtypeStruct((8, 1, width), F32),
            ),
            in_specs=[smem, smem, vmem, vmem, vmem, vmem] + [hbm] * 6,
            out_specs=(vmem, vmem, hbm, vmem),
            scratch_shapes=[
                pltpu.VMEM((24, BLOCK, BLOCK), BF16),
                pltpu.VMEM((table, rows), F32),
                pltpu.VMEM((halo2, rows), BF16),
                pltpu.VMEM((rows, halo2), BF16),
                pltpu.VMEM((8, 1, width), F32),
                pltpu.VMEM((rows, width), F32),
                pltpu.VMEM((rows, width), F32),
                pltpu.VMEM((2, rows, width), F32),
                pltpu.VMEM((2, rows, width), F32),
                pltpu.VMEM((2, rows, 1), F32),
                pltpu.VMEM((2, rows, 1), F32),
                pltpu.VMEM((2, rows, width), BF16),
                pltpu.VMEM((2, rows, width), BF16),
                pltpu.VMEM((rows, width), BF16),
                pltpu.VMEM((width, rows), BF16),
                pltpu.VMEM((2, rows, width), BF16),
                pltpu.VMEM((2, table, 2 * width), BF16),
                pltpu.VMEM((2, HEADS, table, rows), BF16),
                pltpu.VMEM((2, width, rows), BF16),
                pltpu.VMEM((2, 4, rows, BLOCK), BF16),
                pltpu.VMEM((2, 4, rows, BLOCK), BF16),
                pltpu.VMEM((rows, width), BF16),
                pltpu.VMEM((rows, 2 * width), F32),
                pltpu.VMEM((rows, 3 * width), BF16),
                pltpu.VMEM((halo2, 2 * width), BF16),
                pltpu.VMEM((2, halo2, 2 * width), BF16),
                pltpu.VMEM((rows, width), BF16),
                pltpu.VMEM((rows, width), BF16),
                pltpu.SemaphoreType.DMA((3, 12)),
                pltpu.SemaphoreType.DMA((4, 2)),
                pltpu.SemaphoreType.DMA((4, 2)),
                pltpu.SemaphoreType.DMA,
            ],
            compiler_params=pltpu.CompilerParams(
                collective_id=0, has_side_effects=True, vmem_limit_bytes=62 * 2**20
            ),
        )(noise, sizes, send.reshape(1, -1), nbr, cond_w, freq, nodes, qkv, out, up, down, cot)
        grads = lax.psum(grads, ("noise", "patch")).astype(F32)
        phase = jnp.log(noise[0]) * freq[: COND // 2, 0]
        feats = jnp.concatenate([jnp.sin(phase), jnp.cos(phase)])
        cond_grad = lax.psum(
            feats[None, None, :, None] * sums.reshape(2, 4, 1, width), ("noise", "patch")
        )

        def pick(first, count, by_rows):
            layers = jnp.stack([grads[12 + first : 12 + first + count], grads[first : first + count]])
            if not by_rows:
                layers = layers.transpose(0, 2, 1, 3)
            return layers.reshape(2, -1, BLOCK) if by_rows else layers.reshape(2, BLOCK, -1)

        return (
            result,
            igrad,
            pick(9, 3, False),
            pick(8, 1, False),
            pick(4, 4, False),
            pick(0, 4, True),
            cond_grad,
        )

    placed = (
        P("noise", "patch", None),
        P("noise"),
        P("patch"),
        P("patch"),
        P(None, "patch"),
        P(),
        P(),
        P(),
        P(),
        P(),
        P("noise", "patch", None),
    )
    return jax.shard_map(
        shards,
        mesh=mesh,
        in_specs=placed,
        out_specs=(P("noise", "patch", None), P("noise", "patch", None), P(), P(), P(), P(), P()),
        check_vma=False,
    )
```

```python
import functools

import jax
import jax.numpy as jnp
import numpy as np
from jax import lax
from jax.experimental import pallas as pl
from jax.experimental.pallas import tpu as pltpu
from jax.sharding import PartitionSpec as P

HEADS = 4
COND = 32
EPSILON = 1e-05
LOG2E = 1.4426950408889634
MESH = pl.DeviceIdType.MESH
F32 = jnp.float32
BF16 = jnp.bfloat16
BLOCK = 512


def nn(a, b):
    return lax.dot_general(a, b, (((1,), (0,)), ((), ())), preferred_element_type=F32)


def nt(a, b):
    return lax.dot_general(a, b, (((1,), (1,)), ((), ())), preferred_element_type=F32)


def tn(a, b):
    return lax.dot_general(a, b, (((0,), (0,)), ((), ())), preferred_element_type=F32)


def mega(
    patches,
    noise_ref,
    sizes_ref,
    send_ref,
    nbr_ref,
    cond_w_ref,
    freq_ref,
    nodes_hbm,
    qkv_hbm,
    out_hbm,
    up_hbm,
    down_hbm,
    cot_hbm,
    result_ref,
    igrad_ref,
    cond_grad_ref,
    qkv_grad,
    out_grad,
    up_grad,
    down_grad,
    w,
    logc,
    sel,
    sel_t,
    cond,
    hid,
    mid,
    xh1,
    xh2,
    rs1,
    rs2,
    act1,
    act2,
    low,
    tr,
    qv,
    kv,
    prob,
    att_t,
    gate,
    slope,
    dob,
    dkv,
    dqkv,
    rim,
    rin,
    node_in,
    cot_in,
    sums,
    from_core,
    from_one_a,
    from_one_b,
    from_two_a,
    from_two_b,
    from_line,
    sums_in,
    load_sem,
    halo_send,
    halo_recv,
    out_sem,
    rs_send,
    rs_recv,
    ag_send,
    ag_recv,
    sum_send,
    sum_recv,
):
    rows = hid.shape[0]
    table = kv.shape[1]
    halo = rim.shape[0] // 2
    my_noise = lax.axis_index("noise")
    me = lax.axis_index("patch")
    before = (my_noise, lax.rem(me + patches - 1, patches))
    after = (my_noise, lax.rem(me + 1, patches))

    def place(t, k, down, up, out, qkv):
        if k < 4:
            return down.at[t, pl.ds(k * BLOCK, BLOCK), :]
        if k < 8:
            return up.at[t, :, pl.ds((k - 4) * BLOCK, BLOCK)]
        if k < 9:
            return out.at[t]
        return qkv.at[t, :, pl.ds((k - 9) * BLOCK, BLOCK)]

    def load(t, k):
        src = place(t, k, down_hbm, up_hbm, out_hbm, qkv_hbm)
        return pltpu.make_async_copy(src, w.at[(1 - t) * 12 + k], load_sem.at[t, k])

    node_copy = pltpu.make_async_copy(nodes_hbm.at[0], node_in, load_sem.at[2, 0])
    cot_copy = pltpu.make_async_copy(cot_hbm.at[0], cot_in, load_sem.at[2, 1])
    node_copy.start()
    for t in range(2):
        for k in (9, 10, 11, 8, 4, 0, 5, 1, 6, 2, 7, 3):
            load(t, k).start()
    cot_copy.start()

    core = lax.rem(me, 2)
    x = lax.rem(me // 2, 2)
    y = my_noise
    z = me // 4
    line = patches // 4
    core_peer = (my_noise, me + 1 - 2 * core)
    x_peer = (my_noise, me + 2 - 4 * x)
    y_peer = (1 - my_noise, me)

    def line_place(step):
        return lax.rem(z + step, line)

    def line_peer(step):
        return (my_noise, line_place(step) * 4 + lax.rem(me, 4))

    barrier = pltpu.get_barrier_semaphore()
    greeted = [before, after, core_peer, x_peer, y_peer]
    greeted += [line_peer(step) for step in range(1, line)]
    for other in greeted:
        pl.semaphore_signal(barrier, inc=1, device_id=other, device_id_type=MESH)

    step_rows = 64

    def count(i, _):
        base = i * step_rows
        ids = lax.broadcasted_iota(jnp.int32, (step_rows, rows), 0) + base
        total = jnp.zeros((step_rows, rows), F32)
        for j in range(nbr_ref.shape[0]):
            total = total + jnp.where(nbr_ref[j : j + 1, :] == ids, 1.0, 0.0)
        logc[pl.ds(base, step_rows), :] = jnp.where(total > 0.0, jnp.log(total) * LOG2E, -1e30)
        return 0

    lax.fori_loop(0, table // step_rows, count, 0)
    picked = jnp.where(
        lax.broadcasted_iota(jnp.int32, (rows, 2 * halo), 0) == send_ref[...], 1.0, 0.0
    )
    sel_t[...] = picked.astype(BF16)
    sel[...] = picked.T.astype(BF16)

    def features(noise):
        phase = jnp.log(noise) * freq_ref[...]
        is_sin = lax.broadcasted_iota(jnp.int32, (COND, 128), 0) < COND // 2
        feats = jnp.where(is_sin, jnp.sin(phase), jnp.cos(phase))
        return jnp.concatenate([feats] * (hid.shape[1] // 128), axis=1)

    wide = features(jnp.full((COND, 128), noise_ref[0], F32))
    sums[8:16, :] = jnp.full((8, hid.shape[1]), noise_ref[0], F32)
    for t in range(2):
        for i in range(4):
            cond[t * 4 + i] = jnp.sum(cond_w_ref[t, i].astype(F32) * wide, 0, keepdims=True)

    node_copy.wait()
    hid[...] = node_in[...].astype(F32)
    pl.semaphore_wait(barrier, len(greeted))

    head = hid.shape[1] // HEADS
    unit = LOG2E * head ** (-0.5)
    ln_rows = 64

    def norm(value_ref, t, first, normed_ref, inv_ref, out_ref):
        def body(i, _):
            at = pl.ds(i * ln_rows, ln_rows)
            value = value_ref[at, :]
            centred = value - jnp.mean(value, -1, keepdims=True)
            inv = lax.rsqrt(jnp.mean(centred * centred, -1, keepdims=True) + EPSILON)
            normed = centred * inv
            normed_ref[t, at, :] = normed
            inv_ref[t, at, :] = inv
            out_ref[t, at, :] = (
                normed * (1.0 + cond[t * 4 + first]) + cond[t * 4 + first + 1]
            ).astype(BF16)
            return 0

        lax.fori_loop(0, rows // ln_rows, body, 0)

    def halo_copies(stage, src, dst_before, dst_after):
        return [
            pltpu.make_async_remote_copy(
                src_ref=src.at[pl.ds(0, halo)],
                dst_ref=dst_before,
                send_sem=halo_send.at[stage, 0],
                recv_sem=halo_recv.at[stage, 0],
                device_id=before,
                device_id_type=MESH,
            ),
            pltpu.make_async_remote_copy(
                src_ref=src.at[pl.ds(halo, halo)],
                dst_ref=dst_after,
                send_sem=halo_send.at[stage, 1],
                recv_sem=halo_recv.at[stage, 1],
                device_id=after,
                device_id_type=MESH,
            ),
        ]

    def forward(t, _):
        base = (1 - t) * 12
        for k in range(12):
            load_wait(t, k)
        norm(hid, t, 0, xh1, rs1, act1)
        a = act1[t]
        kv[t, pl.ds(0, rows), pl.ds(0, BLOCK)] = nn(a, w[base + 10]).astype(BF16)
        kv[t, pl.ds(0, rows), pl.ds(BLOCK, BLOCK)] = nn(a, w[base + 11]).astype(BF16)
        rim[...] = nn(sel[...], kv[t, pl.ds(0, rows), :]).astype(BF16)
        copies = halo_copies(
            t, rim, kv.at[t, pl.ds(rows + halo, halo), :], kv.at[t, pl.ds(rows, halo), :]
        )
        for copy in copies:
            copy.start()
        qv[t] = nn(a, w[base + 9]).astype(BF16)
        for copy in copies:
            copy.wait()
        for h in range(HEADS):
            keys = kv[t, :, pl.ds(h * head, head)]
            values = kv[t, :, pl.ds(BLOCK + h * head, head)]
            for c in range(2):
                cols = pl.ds(c * 256, 256)
                score = nt(keys, qv[t, cols, pl.ds(h * head, head)]) * unit + logc[:, cols]
                part = jnp.exp2(score - jnp.max(score, 0, keepdims=True))
                weight = (part * (1.0 / jnp.sum(part, 0, keepdims=True))).astype(BF16)
                prob[t, h, :, cols] = weight
                att_t[t, pl.ds(h * head, head), cols] = tn(values, weight).astype(BF16)
        mid[...] = hid[...] + tn(att_t[t], w[base + 8])
        norm(mid, t, 2, xh2, rs2, act2)
        for f in range(4):
            u = nn(act2[t], w[base + 4 + f])
            sig = 0.5 * jnp.tanh(0.5 * u) + 0.5
            g = u * sig
            gate[t, f] = g.astype(BF16)
            slope[t, f] = (sig + g * (1.0 - sig)).astype(BF16)
            if f == 0:
                hid[...] = mid[...] + nn(gate[t, f], w[base + f])
            else:
                hid[...] += nn(gate[t, f], w[base + f])
        return 0

    def load_wait(t, k):
        pltpu.make_async_copy(
            out_hbm.at[0], w.at[(1 - t) * 12 + k], load_sem.at[t, k]
        ).wait()

    lax.fori_loop(0, 2, forward, 0)

    cot_copy.wait()

    def turn(i, _):
        at = pl.ds(i * ln_rows, ln_rows)
        ids = lax.broadcasted_iota(jnp.int32, (ln_rows, hid.shape[1]), 0) + i * ln_rows
        live = ids < sizes_ref[0]
        result_ref[0, at, :] = jnp.where(live, hid[at, :], 0.0).astype(BF16)
        hid[at, :] = jnp.where(live, cot_in[at, :].astype(F32), 0.0)
        return 0

    lax.fori_loop(0, rows // ln_rows, turn, 0)

    def norm_back(t, first, grad_ref, normed_ref, inv_ref, add_ref, out_ref):
        def body(i, carry):
            scale_sum, shift_sum = carry
            at = pl.ds(i * ln_rows, ln_rows)
            grad = grad_ref[at, :]
            normed = normed_ref[t, at, :]
            back = grad * normed
            scale_sum = scale_sum + jnp.sum(back, 0, keepdims=True)
            shift_sum = shift_sum + jnp.sum(grad, 0, keepdims=True)
            scaled = grad * (1.0 + cond[t * 4 + first])
            one = jnp.mean(scaled, -1, keepdims=True)
            two = jnp.mean(scaled * normed, -1, keepdims=True)
            out = add_ref[at, :] + inv_ref[t, at, :] * (scaled - one - normed * two)
            out_ref[at, :] = out
            low[at, :] = out.astype(BF16)
            return scale_sum, shift_sum

        zero = jnp.zeros((1, hid.shape[1]), F32)
        scale_sum, shift_sum = lax.fori_loop(0, rows // ln_rows, body, (zero, zero))
        sums[pl.ds(t * 4 + first, 1), :] = scale_sum
        sums[pl.ds(t * 4 + first + 1, 1), :] = shift_sum

    slots = from_core.shape[0]
    half, quarter, eighth = BLOCK // 2, BLOCK // 4, BLOCK // 8
    line_rows = min(line, 4)
    piece_rows, piece_cols = eighth // line_rows, BLOCK * line_rows // line
    left, right = pl.ds(0, half), pl.ds(half, half)
    mine = core * half + x * quarter + y * eighth

    def strip(start, size):
        return pl.ds(pl.multiple_of(start, 16), size)

    def piece(n, place_on_line):
        at = strip(mine + lax.rem(place_on_line, line_rows) * piece_rows, piece_rows)
        if line <= 4:
            return (n, at, pl.ds(0, BLOCK))
        first = (place_on_line // line_rows) * piece_cols
        return (n, at, pl.ds(pl.multiple_of(first, 128), piece_cols))

    def remote(src, dst, sems, which, n, peer):
        slot = lax.rem(n, slots)
        return pltpu.make_async_remote_copy(
            src_ref=src,
            dst_ref=dst,
            send_sem=sems[0].at[which, slot],
            recv_sem=sems[1].at[which, slot],
            device_id=peer,
            device_id_type=MESH,
        )

    rs = (rs_send, rs_recv)
    ag = (ag_send, ag_recv)

    def send_core(n):
        src = w.at[n, strip((1 - core) * half, half), :]
        return [remote(src, from_core.at[lax.rem(n, slots)], rs, 0, n, core_peer)]

    def send_one(n):
        slot = lax.rem(n, slots)
        src = w.at[n, strip(core * half + (1 - x) * quarter, quarter), left]
        copies = [remote(src, from_one_a.at[slot], rs, 1, n, x_peer)]
        for i in range(2):
            src = w.at[n, strip(core * half + i * quarter + (1 - y) * eighth, eighth), right]
            dst = from_one_b.at[slot, pl.ds(i * eighth, eighth)]
            copies.append(remote(src, dst, rs, 2 + i, n, y_peer))
        return copies

    def send_two(n):
        slot = lax.rem(n, slots)
        src_a = w.at[n, strip(core * half + x * quarter + (1 - y) * eighth, eighth), left]
        src_b = w.at[n, strip(core * half + (1 - x) * quarter + y * eighth, eighth), right]
        return [
            remote(src_a, from_two_a.at[slot], rs, 4, n, y_peer),
            remote(src_b, from_two_b.at[slot], rs, 5, n, x_peer),
        ]

    def send_line(n):
        slot = lax.rem(n, slots)
        return [
            remote(
                w.at[piece(n, line_place(step))],
                from_line.at[slot, step - 1],
                rs,
                5 + step,
                n,
                line_peer(step),
            )
            for step in range(1, line)
        ]

    def start(copies):
        for copy in copies:
            copy.start()

    def finish(copies):
        for copy in copies:
            copy.wait()

    def add(n, rows_at, cols, other):
        total = w[n, rows_at, cols].astype(F32) + other.astype(F32)
        w[n, rows_at, cols] = total.astype(BF16)

    def after_core(n):
        finish(send_core(n))
        slot = lax.rem(n, slots)
        for i in range(2):
            at = strip(core * half + i * quarter, quarter)
            add(n, at, pl.ds(0, BLOCK), from_core[slot, pl.ds(i * quarter, quarter)])
        start(send_one(n))

    def after_one(n):
        finish(send_one(n))
        slot = lax.rem(n, slots)
        add(n, strip(core * half + x * quarter, quarter), left, from_one_a[slot])
        for i in range(2):
            at = strip(core * half + i * quarter + y * eighth, eighth)
            add(n, at, right, from_one_b[slot, pl.ds(i * eighth, eighth)])
        start(send_two(n))

    def after_two(n):
        finish(send_two(n))
        slot = lax.rem(n, slots)
        add(n, strip(mine, eighth), left, from_two_a[slot])
        add(n, strip(mine, eighth), right, from_two_b[slot])
        start(send_line(n))

    def after_line(n):
        finish(send_line(n))
        slot = lax.rem(n, slots)
        at = piece(n, z)
        total = w[at].astype(F32)
        for step in range(1, line):
            total = total + from_line[slot, step - 1].astype(F32)
        w[at] = total.astype(BF16)

    def spread_line(n):
        own = w.at[piece(n, z)]
        return [
            remote(own, own, ag, 5 + step, n, line_peer(step)) for step in range(1, line)
        ]

    def spread_two(n):
        a = w.at[n, strip(mine, eighth), left]
        b = w.at[n, strip(mine, eighth), right]
        return [remote(a, a, ag, 4, n, y_peer), remote(b, b, ag, 5, n, x_peer)]

    def spread_one(n):
        own = w.at[n, strip(core * half + x * quarter, quarter), left]
        copies = [remote(own, own, ag, 1, n, x_peer)]
        for i in range(2):
            own = w.at[n, strip(core * half + i * quarter + y * eighth, eighth), right]
            copies.append(remote(own, own, ag, 2 + i, n, y_peer))
        return copies

    def spread_core(n):
        own = w.at[n, strip(core * half, half), :]
        return [remote(own, own, ag, 0, n, core_peer)]

    def write_out(n):
        def by_kind(k, t):
            for low_k, high_k in ((0, 4), (4, 8), (8, 9), (9, 12)):

                @pl.when((k >= low_k) & (k < high_k))
                def _():
                    at = pl.ds(pl.multiple_of((k - low_k) * BLOCK, BLOCK), BLOCK)
                    dst = {
                        0: down_grad.at[t, at, :],
                        4: up_grad.at[t, :, at],
                        8: out_grad.at[t],
                        9: qkv_grad.at[t, :, at],
                    }[low_k]
                    pltpu.make_async_copy(w.at[n], dst, out_sem.at[n]).start()

        by_kind(lax.rem(n, 12), 1 - n // 12)

    blocks = 24
    rs_lag = 2
    ag_lag = 2

    def when_block(n, act):
        @pl.when((n >= 0) & (n < blocks))
        def _():
            act(n)

    def reduce_tick(k):
        when_block(k, lambda n: start(send_core(n)))
        when_block(k - rs_lag, after_core)
        when_block(k - 2 * rs_lag, after_one)
        when_block(k - 3 * rs_lag, after_two)
        when_block(k - 4 * rs_lag, after_line)

    def spread_tick(a):
        def after_spread_line(n):
            finish(spread_line(n))
            start(spread_two(n))

        def after_spread_two(n):
            finish(spread_two(n))
            start(spread_one(n))

        def after_spread_one(n):
            finish(spread_one(n))
            start(spread_core(n))

        def after_spread_core(n):
            finish(spread_core(n))
            write_out(n)

        when_block(a, lambda n: start(spread_line(n)))
        when_block(a - ag_lag, after_spread_line)
        when_block(a - 2 * ag_lag, after_spread_two)
        when_block(a - 3 * ag_lag, after_spread_one)
        when_block(a - 4 * ag_lag, after_spread_core)

    low[...] = hid[...].astype(BF16)

    def backward(i, _):
        t = 1 - i
        base = i * 12
        for f in range(4):
            slope[t, f] = (nt(low[...], w[base + f]) * slope[t, f].astype(F32)).astype(BF16)
        for f in range(4):
            w[base + f] = tn(gate[t, f], low[...]).astype(BF16)
            reduce_tick(base + f)
            if f == 0:
                mid[...] = nt(slope[t, f], w[base + 4 + f])
            else:
                mid[...] += nt(slope[t, f], w[base + 4 + f])
        norm_back(t, 2, mid, xh2, rs2, hid, mid)
        dob[...] = nt(low[...], w[base + 8]).astype(BF16)
        tr[...] = act2[t].T
        for h in range(HEADS):
            lanes = pl.ds(h * head, head)
            keys = kv[t, :, lanes]
            values = kv[t, :, pl.ds(BLOCK + h * head, head)]
            weight = prob[t, h]
            grad_out = dob[:, lanes]
            grad_weight = nt(values, grad_out)
            spread = weight.astype(F32) * grad_weight
            delta = jnp.sum(spread, 0, keepdims=True)
            ds = (spread - weight.astype(F32) * delta).astype(BF16)
            dv = nn(weight, grad_out)
            dk = nn(ds, qv[t, :, lanes]) * (head ** (-0.5))
            dq_t = tn(keys, ds) * (head ** (-0.5))
            dqkv[:, lanes] = dq_t.T.astype(BF16)
            dkv[:, lanes] = dk[:rows]
            dkv[:, pl.ds(BLOCK + h * head, head)] = dv[:rows]
            rim[:, lanes] = dk[rows:].astype(BF16)
            rim[:, pl.ds(BLOCK + h * head, head)] = dv[rows:].astype(BF16)
            w[base + 4 + h] = nn(tr[...], slope[t, h]).astype(BF16)
            reduce_tick(base + 4 + h)
        copies = halo_copies(
            2 + t, rim, rin.at[t, pl.ds(halo, halo), :], rin.at[t, pl.ds(0, halo), :]
        )
        for copy in copies:
            copy.start()
        w[base + 8] = nn(att_t[t], low[...]).astype(BF16)
        reduce_tick(base + 8)
        tr[...] = act1[t].T
        back = nt(dqkv[:, pl.ds(0, BLOCK)], w[base + 9])
        w[base + 9] = nn(tr[...], dqkv[:, pl.ds(0, BLOCK)]).astype(BF16)
        hid[...] = back
        reduce_tick(base + 9)
        for copy in copies:
            copy.wait()
        dqkv[:, pl.ds(BLOCK, 2 * BLOCK)] = (dkv[...] + nn(sel_t[...], rin[t])).astype(BF16)
        for k in range(1, 3):
            hid[...] += nt(dqkv[:, pl.ds(k * BLOCK, BLOCK)], w[base + 9 + k])
            w[base + 9 + k] = nn(tr[...], dqkv[:, pl.ds(k * BLOCK, BLOCK)]).astype(BF16)
            reduce_tick(base + 9 + k)
        norm_back(t, 0, hid, xh1, rs1, mid, hid)
        return 0

    lax.fori_loop(0, 2, backward, 0)
    igrad_ref[0] = hid[...]

    def sum_copy(which, src, dst, peer):
        return pltpu.make_async_remote_copy(
            src_ref=src,
            dst_ref=dst,
            send_sem=sum_send.at[which],
            recv_sem=sum_recv.at[which],
            device_id=peer,
            device_id_type=MESH,
        )

    own_sums = sums.at[pl.ds(0, 8)]
    sum_stages = [
        [sum_copy(0, own_sums, sums_in.at[0, pl.ds(0, 8)], core_peer)],
        [sum_copy(1, own_sums, sums_in.at[1, pl.ds(0, 8)], x_peer)],
        [
            sum_copy(1 + step, own_sums, sums_in.at[1 + step, pl.ds(0, 8)], line_peer(step))
            for step in range(1, line)
        ],
        [sum_copy(1 + line, sums, sums_in.at[1 + line], y_peer)],
    ]

    def drain(first, last):
        def body(k, _):
            spread_tick(k - blocks)
            reduce_tick(k)
            return 0

        lax.fori_loop(first, last, body, 0)

    start(sum_stages[0])
    at_tick = blocks
    for stage in range(4):
        drain(at_tick, at_tick + 6)
        at_tick += 6
        finish(sum_stages[stage])
        if stage < 3:
            got = {0: [0], 1: [1], 2: list(range(2, 1 + line))}[stage]
            total = sums[0:8, :]
            for g in got:
                total = total + sums_in[g, 0:8, :]
            sums[0:8, :] = total
            start(sum_stages[stage + 1])
    other = features(jnp.concatenate([sums_in[1 + line, 8:16, 0:128]] * (COND // 8), axis=0))
    for t in range(2):
        for i in range(4):
            row = pl.ds(t * 4 + i, 1)
            cond_grad_ref[t, i] = wide * sums[row, :] + other * sums_in[1 + line, row, :]
    drain(at_tick, 2 * blocks + 4 * ag_lag)

    def settle(n, _):
        pltpu.make_async_copy(w.at[n], out_grad.at[0], out_sem.at[n]).wait()
        return 0

    lax.fori_loop(0, blocks, settle, 0)


def solution(mesh):
    patches = mesh.shape["patch"]

    def shards(nodes, noise, sizes, send, nbr, qkv, out, up, down, cond_w, cot):
        rows, width = nodes.shape[1:]
        halo2 = send.shape[0]
        halo = halo2 // 2
        table = rows + halo2
        freq = np.tile(2.0 ** (np.arange(COND) % (COND // 2) / 4.0), (128, 1)).T.astype(np.float32)
        vmem = pl.BlockSpec(memory_space=pltpu.VMEM)
        smem = pl.BlockSpec(memory_space=pltpu.SMEM)
        hbm = pl.BlockSpec(memory_space=pl.ANY)
        line = patches // 4
        slots = 8
        piece = (BLOCK // 8 // min(line, 4), BLOCK * min(line, 4) // line)
        result, igrad, cond_grad, *grads = pl.pallas_call(
            functools.partial(mega, patches),
            out_shape=(
                jax.ShapeDtypeStruct((1, rows, width), BF16),
                jax.ShapeDtypeStruct((1, rows, width), F32),
                jax.ShapeDtypeStruct(cond_w.shape, F32),
                *(jax.ShapeDtypeStruct(v.shape, BF16) for v in (qkv, out, up, down)),
            ),
            in_specs=[smem, smem, vmem, vmem, vmem, vmem] + [hbm] * 6,
            out_specs=(vmem, vmem, vmem, hbm, hbm, hbm, hbm),
            scratch_shapes=[
                pltpu.VMEM((24, BLOCK, BLOCK), BF16),
                pltpu.VMEM((table, rows), F32),
                pltpu.VMEM((halo2, rows), BF16),
                pltpu.VMEM((rows, halo2), BF16),
                pltpu.VMEM((8, 1, width), F32),
                pltpu.VMEM((rows, width), F32),
                pltpu.VMEM((rows, width), F32),
                pltpu.VMEM((2, rows, width), F32),
                pltpu.VMEM((2, rows, width), F32),
                pltpu.VMEM((2, rows, 1), F32),
                pltpu.VMEM((2, rows, 1), F32),
                pltpu.VMEM((2, rows, width), BF16),
                pltpu.VMEM((2, rows, width), BF16),
                pltpu.VMEM((rows, width), BF16),
                pltpu.VMEM((width, rows), BF16),
                pltpu.VMEM((2, rows, width), BF16),
                pltpu.VMEM((2, table, 2 * width), BF16),
                pltpu.VMEM((2, HEADS, table, rows), BF16),
                pltpu.VMEM((2, width, rows), BF16),
                pltpu.VMEM((2, 4, rows, BLOCK), BF16),
                pltpu.VMEM((2, 4, rows, BLOCK), BF16),
                pltpu.VMEM((rows, width), BF16),
                pltpu.VMEM((rows, 2 * width), F32),
                pltpu.VMEM((rows, 3 * width), BF16),
                pltpu.VMEM((halo2, 2 * width), BF16),
                pltpu.VMEM((2, halo2, 2 * width), BF16),
                pltpu.VMEM((rows, width), BF16),
                pltpu.VMEM((rows, width), BF16),
                pltpu.VMEM((16, width), F32),
                pltpu.VMEM((slots, BLOCK // 2, BLOCK), BF16),
                pltpu.VMEM((slots, BLOCK // 4, BLOCK // 2), BF16),
                pltpu.VMEM((slots, BLOCK // 4, BLOCK // 2), BF16),
                pltpu.VMEM((slots, BLOCK // 8, BLOCK // 2), BF16),
                pltpu.VMEM((slots, BLOCK // 8, BLOCK // 2), BF16),
                pltpu.VMEM((slots, line - 1, *piece), BF16),
                pltpu.VMEM((2 + line, 16, width), F32),
                pltpu.SemaphoreType.DMA((3, 12)),
                pltpu.SemaphoreType.DMA((4, 2)),
                pltpu.SemaphoreType.DMA((4, 2)),
                pltpu.SemaphoreType.DMA((24,)),
                pltpu.SemaphoreType.DMA((5 + line, slots)),
                pltpu.SemaphoreType.DMA((5 + line, slots)),
                pltpu.SemaphoreType.DMA((5 + line, slots)),
                pltpu.SemaphoreType.DMA((5 + line, slots)),
                pltpu.SemaphoreType.DMA((2 + line,)),
                pltpu.SemaphoreType.DMA((2 + line,)),
            ],
            compiler_params=pltpu.CompilerParams(
                collective_id=0, has_side_effects=True, vmem_limit_bytes=62 * 2**20
            ),
        )(noise, sizes, send.reshape(1, -1), nbr, cond_w, freq, nodes, qkv, out, up, down, cot)
        return (result, igrad, *(grad.astype(F32) for grad in grads), cond_grad)

    placed = (
        P("noise", "patch", None),
        P("noise"),
        P("patch"),
        P("patch"),
        P(None, "patch"),
        P(),
        P(),
        P(),
        P(),
        P(),
        P("noise", "patch", None),
    )
    return jax.shard_map(
        shards,
        mesh=mesh,
        in_specs=placed,
        out_specs=(P("noise", "patch", None), P("noise", "patch", None), P(), P(), P(), P(), P()),
        check_vma=False,
    )
```

```python
import functools

import jax
import jax.numpy as jnp
import numpy as np
from jax import lax
from jax.experimental import pallas as pl
from jax.experimental.pallas import tpu as pltpu
from jax.sharding import PartitionSpec as P

HEADS = 4
COND = 32
SLOTS = 16
EPSILON = 1e-05
LOG2E = 1.4426950408889634
MESH = pl.DeviceIdType.MESH
F32 = jnp.float32
BF16 = jnp.bfloat16
BLOCK = 512


WHOLE, LEFT, RIGHT = (0, BLOCK), (0, BLOCK // 2), (BLOCK // 2, BLOCK // 2)


def square(row, size, x, y, last):
    one, two = size // 2, size // 4
    first = [(row + x * one, row + (1 - x) * one, one, LEFT, LEFT, 0, LEFT, "x")]
    second = []
    for i in range(2):
        at = row + i * one
        first.append((at + y * two, at + (1 - y) * two, two, RIGHT, RIGHT, i * two, RIGHT, "y"))
        if last:
            second.append((at + y * two, at + y * two, two, RIGHT, RIGHT, i * two, RIGHT, "x"))
    mine = row + x * one
    kept = mine + y * two
    if last:
        second.append((mine, mine, one, LEFT, LEFT, 0, LEFT, "y"))
    else:
        second.append((kept, mine + (1 - y) * two, two, LEFT, LEFT, 0, LEFT, "y"))
        other = row + (1 - x) * one + y * two
        second.append((kept, other, two, RIGHT, RIGHT, 0, RIGHT, "x"))
    return kept, two, first, second


def along_line(row, size, cols, bit, b, last):
    if last:
        return (row, size, cols), [(row, row, size, cols, cols, 0, (0, cols[1]), b)]
    if size >= 32:
        size //= 2
        keep, send = row + bit * size, row + (1 - bit) * size
        return (keep, size, cols), [(keep, send, size, cols, cols, 0, (0, cols[1]), b)]
    first, width = cols[0], cols[1] // 2
    keep, send = (first + bit * width, width), (first + (1 - bit) * width, width)
    return (row, size, keep), [(row, row, size, keep, send, 0, (0, width), b)]


def exchanges(core, x, y, bits, line_first):
    half = BLOCK // 2
    row, size, cols = core * half, half, WHOLE
    out = [[(row, (1 - core) * half, half, WHOLE, WHOLE, 0, WHOLE, "core")]]
    if not line_first:
        row, size, first, second = square(row, size, x, y, False)
        out += [first, second]
    for b, bit in enumerate(bits):
        last = not line_first and b == len(bits) - 1
        (row, size, cols), parts = along_line(row, size, cols, bit, b, last)
        out.append(parts)
    if line_first:
        row, size, first, second = square(row, size, x, y, True)
        out += [first, second]
    return out


LINE_FIRST = (5, 13, 18, 21)


def goes_line_first(n, line_bits):
    return line_bits == 2 and n in LINE_FIRST


PIECES = (
    *((f"down{f}", 0.6, f) for f in range(4)),
    *((f"feed{f}", 0.3, None) for f in range(4)),
    ("norm2", 1.0, None),
    ("attended", 0.3, None),
    *(p for h in range(4) for p in ((f"head{h}", 0.75, None), (f"up{h}", 0.3, 4 + h))),
    ("halo", 0.1, None),
    ("out", 0.3, 8),
    ("query", 1.0, 9),
    ("table", 0.5, None),
    ("key", 0.6, 10),
    ("value", 0.6, 11),
    ("norm1", 0.9, None),
)
REDUCE_LAGS = ((2, 3, 3, 3, 3), (1, 3, 3, 2, 5))
GATHER_LAGS = ((2, 5, 7, 3), (4, 4, 7, 2))
GATHER_WAIT = (1, 1)
SUMS_LAG = 3


def schedule(line_bits, slots):
    tables = [exchanges(0, 0, 0, [0] * line_bits, f) for f in (False, True)]
    stages = 3 + line_bits
    sum_dirs = ["core", "x", *range(line_bits), "y"]

    def dirs_of(kind, s, n):
        if kind == "sums":
            return {sum_dirs[s]}
        return {p[7] for p in tables[goes_line_first(n, line_bits)][s]}

    order, sent, seen = [], [], set()
    reduced = {}
    places = {}

    def told(since, dirs):
        return all(
            any(at > since and d in ds and key in seen for at, ds, key in sent) for d in dirs
        )

    def find_slot(kind, s, dirs):
        for slot in range(slots):
            since = places.get((kind, s, slot), -1)
            if since == -1 or (since is not None and told(since, dirs)):
                return slot
        return None

    def lag(kind, s, n):
        if kind == "sums":
            return SUMS_LAG
        lags = (REDUCE_LAGS if kind == "reduce" else GATHER_LAGS)[goes_line_first(n, line_bits)]
        if kind == "reduce":
            return lags[min(s, len(lags) - 1)]
        return lags[max(0, len(lags) - 1 - s)]

    flying, waiting = [], []

    def start_due(turn):
        for item in sorted(v for v in waiting if v[0] <= turn):
            _, kind, s, n = item
            dirs = dirs_of(kind, s, n)
            if kind == "gather" and not told(reduced[s, n], dirs):
                continue
            slot = 0 if kind == "sums" else find_slot(kind, s, dirs)
            if slot is None:
                continue
            waiting.remove(item)
            order.append(("send", kind, s, n, slot))
            places[kind, s, slot] = None
            sent.append((len(order), dirs, (kind, s, n)))
            flying.append((turn + lag(kind, s, n), kind, s, n, slot))

    def take_turn(turn):
        due = [v for v in flying if v[0] <= turn]
        rank = {"gather": 0, "sums": 1, "reduce": 2}
        due.sort(key=lambda v: (rank[v[1]], v[2] if v[1] == "gather" else -v[2], v[3]))
        for item in due:
            flying.remove(item)
            _, kind, s, n, slot = item
            order.append(("take", kind, s, n, slot))
            seen.add((kind, s, n))
            places[kind, s, slot] = len(order)
            if kind == "reduce":
                reduced[s, n] = len(order)
                if s + 1 < stages:
                    waiting.append((turn, kind, s + 1, n))
                else:
                    wait = GATHER_WAIT[goes_line_first(n, line_bits)]
                    waiting.append((turn + wait, "gather", s - 1, n))
            elif kind == "gather" and s > 0:
                waiting.append((turn, kind, s - 1, n))
            elif kind == "sums" and s + 1 < len(sum_dirs):
                waiting.append((turn, kind, s + 1, n))
            start_due(turn)
        start_due(turn)

    turn = 0
    for i in range(2):
        for name, _, made in PIECES:
            order.append(("work", name, i))
            if made is not None:
                waiting.append((turn, "reduce", 0, i * 12 + made))
                take_turn(turn)
                turn += 1
    waiting.append((turn, "sums", 0, 0))
    while flying or waiting:
        before = len(order)
        take_turn(turn)
        turn += 1
        if len(order) == before and not flying:
            for d in dirs_of(*waiting[0][1:]):
                order += [("send", "token", d, 0, 0), ("take", "token", d, 0, 0)]
                sent.append((len(order), {d}, ("token", len(order))))
                seen.add(("token", len(order)))
    return order


def nn(a, b):
    return lax.dot_general(a, b, (((1,), (0,)), ((), ())), preferred_element_type=F32)


def nt(a, b):
    return lax.dot_general(a, b, (((1,), (1,)), ((), ())), preferred_element_type=F32)


def tn(a, b):
    return lax.dot_general(a, b, (((0,), (0,)), ((), ())), preferred_element_type=F32)


def mega(
    patches,
    order,
    noise_ref,
    sizes_ref,
    send_ref,
    nbr_ref,
    cond_w_ref,
    freq_ref,
    nodes_hbm,
    qkv_hbm,
    out_hbm,
    up_hbm,
    down_hbm,
    cot_hbm,
    result_ref,
    igrad_ref,
    cond_grad_ref,
    w,
    logc,
    sel,
    sel_t,
    cond,
    hid,
    mid,
    xh1,
    xh2,
    rs1,
    rs2,
    act1,
    act2,
    low,
    tr,
    qv,
    kv,
    prob,
    att_t,
    gate,
    slope,
    dob,
    dkv,
    dqkv,
    rim,
    rin,
    node_in,
    cot_in,
    sums,
    stat,
    sums_in,
    load_sem,
    halo_send,
    halo_recv,
    rs_send,
    rs_recv,
    ag_send,
    ag_recv,
    sum_send,
    sum_recv,
    token,
    *inbox,
):
    rows = hid.shape[0]
    table = kv.shape[1]
    halo = rim.shape[0] // 2
    my_noise = lax.axis_index("noise")
    me = lax.axis_index("patch")
    before = (my_noise, lax.rem(me + patches - 1, patches))
    after = (my_noise, lax.rem(me + 1, patches))

    def place(t, k, down, up, out, qkv):
        if k < 4:
            return down.at[t, pl.ds(k * BLOCK, BLOCK), :]
        if k < 8:
            return up.at[t, :, pl.ds((k - 4) * BLOCK, BLOCK)]
        if k < 9:
            return out.at[t]
        return qkv.at[t, :, pl.ds((k - 9) * BLOCK, BLOCK)]

    def load(t, k):
        src = place(t, k, down_hbm, up_hbm, out_hbm, qkv_hbm)
        return pltpu.make_async_copy(src, w.at[(1 - t) * 12 + k], load_sem.at[t, k])

    node_copy = pltpu.make_async_copy(nodes_hbm.at[0], node_in, load_sem.at[2, 0])
    cot_copy = pltpu.make_async_copy(cot_hbm.at[0], cot_in, load_sem.at[2, 1])
    node_copy.start()
    for t in range(2):
        for k in (9, 10, 11, 8, 4, 0, 5, 1, 6, 2, 7, 3):
            load(t, k).start()
    cot_copy.start()

    core = lax.rem(me, 2)
    x = lax.rem(me // 2, 2)
    y = my_noise
    z = me // 4
    line = patches // 4
    core_peer = (my_noise, me + 1 - 2 * core)
    x_peer = (my_noise, me + 2 - 4 * x)
    y_peer = (1 - my_noise, me)

    barrier = pltpu.get_barrier_semaphore()
    greeted = [before, after, core_peer, x_peer, y_peer]
    for b in range(line.bit_length() - 1):
        bit = lax.rem(z // (1 << b), 2)
        greeted.append((my_noise, me + 4 * (1 << b) * (1 - 2 * bit)))
    for other in greeted:
        pl.semaphore_signal(barrier, inc=1, device_id=other, device_id_type=MESH)

    step_rows = 64

    def count(i, _):
        base = i * step_rows
        ids = lax.broadcasted_iota(jnp.int32, (step_rows, rows), 0) + base
        total = jnp.zeros((step_rows, rows), F32)
        for j in range(nbr_ref.shape[0]):
            total = total + jnp.where(nbr_ref[j : j + 1, :] == ids, 1.0, 0.0)
        logc[pl.ds(base, step_rows), :] = jnp.where(total > 0.0, jnp.log(total) * LOG2E, -1e30)
        return 0

    lax.fori_loop(0, table // step_rows, count, 0)
    picked = jnp.where(
        lax.broadcasted_iota(jnp.int32, (rows, 2 * halo), 0) == send_ref[...], 1.0, 0.0
    )
    sel_t[...] = picked.astype(BF16)
    sel[...] = picked.T.astype(BF16)

    def features(noise):
        phase = jnp.log(noise) * freq_ref[...]
        is_sin = lax.broadcasted_iota(jnp.int32, (COND, 128), 0) < COND // 2
        feats = jnp.where(is_sin, jnp.sin(phase), jnp.cos(phase))
        return jnp.concatenate([feats] * (hid.shape[1] // 128), axis=1)

    wide = features(jnp.full((COND, 128), noise_ref[0], F32))
    sums[8:16, :] = jnp.full((8, hid.shape[1]), noise_ref[0], F32)
    for t in range(2):
        for i in range(4):
            cond[t * 4 + i] = jnp.sum(cond_w_ref[t, i].astype(F32) * wide, 0, keepdims=True)

    node_copy.wait()
    hid[...] = node_in[...].astype(F32)
    pl.semaphore_wait(barrier, len(greeted))

    head = hid.shape[1] // HEADS
    unit = LOG2E * head ** (-0.5)
    ln_rows = 64

    def norm(value_ref, t, first, normed_ref, inv_ref, out_ref):
        def body(i, _):
            at = pl.ds(i * ln_rows, ln_rows)
            value = value_ref[at, :]
            centred = value - jnp.mean(value, -1, keepdims=True)
            inv = lax.rsqrt(jnp.mean(centred * centred, -1, keepdims=True) + EPSILON)
            normed = centred * inv
            normed_ref[t, at, :] = normed
            inv_ref[t, at, :] = inv
            out_ref[t, at, :] = (
                normed * (1.0 + cond[t * 4 + first]) + cond[t * 4 + first + 1]
            ).astype(BF16)
            return 0

        lax.fori_loop(0, rows // ln_rows, body, 0, unroll=4)

    def halo_copies(stage, src, dst_before, dst_after):
        return [
            pltpu.make_async_remote_copy(
                src_ref=src.at[pl.ds(0, halo)],
                dst_ref=dst_before,
                send_sem=halo_send.at[stage, 0],
                recv_sem=halo_recv.at[stage, 0],
                device_id=before,
                device_id_type=MESH,
            ),
            pltpu.make_async_remote_copy(
                src_ref=src.at[pl.ds(halo, halo)],
                dst_ref=dst_after,
                send_sem=halo_send.at[stage, 1],
                recv_sem=halo_recv.at[stage, 1],
                device_id=after,
                device_id_type=MESH,
            ),
        ]

    def forward(t, _):
        base = (1 - t) * 12
        for k in range(12):
            load_wait(t, k)
        norm(hid, t, 0, xh1, rs1, act1)
        a = act1[t]
        kv[t, pl.ds(0, rows), pl.ds(0, BLOCK)] = nn(a, w[base + 10]).astype(BF16)
        kv[t, pl.ds(0, rows), pl.ds(BLOCK, BLOCK)] = nn(a, w[base + 11]).astype(BF16)
        rim[...] = nn(sel[...], kv[t, pl.ds(0, rows), :]).astype(BF16)
        copies = halo_copies(
            t, rim, kv.at[t, pl.ds(rows + halo, halo), :], kv.at[t, pl.ds(rows, halo), :]
        )
        for copy in copies:
            copy.start()
        qv[t] = nn(a, w[base + 9]).astype(BF16)
        own, far = pl.ds(0, rows), pl.ds(rows, table - rows)
        for h in range(HEADS):
            lanes = pl.ds(h * head, head)
            for c in range(2):
                cols = pl.ds(c * 256, 256)
                score = nt(kv[t, own, lanes], qv[t, cols, lanes]) * unit + logc[own, cols]
                top = jnp.max(score, 0, keepdims=True)
                part = jnp.exp2(score - top)
                prob[t, h, own, cols] = part.astype(BF16)
                stat[2 * h : 2 * h + 1, cols] = top
                stat[2 * h + 1 : 2 * h + 2, cols] = jnp.sum(part, 0, keepdims=True)
        for copy in copies:
            copy.wait()
        for h in range(HEADS):
            lanes = pl.ds(h * head, head)
            score = nt(kv[t, far, lanes], qv[t, :, lanes]) * unit + logc[far, :]
            near_top = stat[2 * h : 2 * h + 1, :]
            top = jnp.maximum(near_top, jnp.max(score, 0, keepdims=True))
            part = jnp.exp2(score - top)
            scale = jnp.exp2(near_top - top)
            inv = 1.0 / (stat[2 * h + 1 : 2 * h + 2, :] * scale + jnp.sum(part, 0, keepdims=True))
            prob[t, h, far, :] = (part * inv).astype(BF16)
            prob[t, h, own, :] = (prob[t, h, own, :].astype(F32) * (scale * inv)).astype(BF16)
            values = kv[t, :, pl.ds(BLOCK + h * head, head)]
            att_t[t, lanes, :] = tn(values, prob[t, h]).astype(BF16)
        mid[...] = hid[...] + tn(att_t[t], w[base + 8])
        norm(mid, t, 2, xh2, rs2, act2)
        for f in range(4):
            u = nn(act2[t], w[base + 4 + f])
            sig = 0.5 * jnp.tanh(0.5 * u) + 0.5
            g = u * sig
            gate[t, f] = g.astype(BF16)
            slope[t, f] = (sig + g * (1.0 - sig)).astype(BF16)
            if f == 0:
                hid[...] = mid[...] + nn(gate[t, f], w[base + f])
            else:
                hid[...] += nn(gate[t, f], w[base + f])
        return 0

    def load_wait(t, k):
        pltpu.make_async_copy(
            out_hbm.at[0], w.at[(1 - t) * 12 + k], load_sem.at[t, k]
        ).wait()

    lax.fori_loop(0, 2, forward, 0)

    cot_copy.wait()

    def turn(i, _):
        at = pl.ds(i * ln_rows, ln_rows)
        ids = lax.broadcasted_iota(jnp.int32, (ln_rows, hid.shape[1]), 0) + i * ln_rows
        live = ids < sizes_ref[0]
        result_ref[0, at, :] = jnp.where(live, hid[at, :], 0.0).astype(BF16)
        hid[at, :] = jnp.where(live, cot_in[at, :].astype(F32), 0.0)
        return 0

    lax.fori_loop(0, rows // ln_rows, turn, 0)

    def norm_back(t, first, grad_ref, normed_ref, inv_ref, add_ref, out_ref):
        def body(i, carry):
            scale_sum, shift_sum = carry
            at = pl.ds(i * ln_rows, ln_rows)
            grad = grad_ref[at, :]
            normed = normed_ref[t, at, :]
            back = grad * normed
            scale_sum = scale_sum + jnp.sum(back.reshape(-1, 8, hid.shape[1]), 0)
            shift_sum = shift_sum + jnp.sum(grad.reshape(-1, 8, hid.shape[1]), 0)
            scaled = grad * (1.0 + cond[t * 4 + first])
            one = jnp.mean(scaled, -1, keepdims=True)
            two = jnp.mean(scaled * normed, -1, keepdims=True)
            out = add_ref[at, :] + inv_ref[t, at, :] * (scaled - one - normed * two)
            out_ref[at, :] = out
            low[at, :] = out.astype(BF16)
            return scale_sum, shift_sum

        zero = jnp.zeros((8, hid.shape[1]), F32)
        scale_sum, shift_sum = lax.fori_loop(0, rows // ln_rows, body, (zero, zero), unroll=4)
        sums[pl.ds(t * 4 + first, 1), :] = jnp.sum(scale_sum, 0, keepdims=True)
        sums[pl.ds(t * 4 + first + 1, 1), :] = jnp.sum(shift_sum, 0, keepdims=True)

    bits = [lax.rem(z // (1 << b), 2) for b in range(line.bit_length() - 1)]
    stages = 3 + len(bits)
    plans = [exchanges(core, x, y, bits, f) for f in (False, True)]
    peers = {"core": core_peer, "x": x_peer, "y": y_peer}
    for b, bit in enumerate(bits):
        peers[b] = (my_noise, me + 4 * (1 << b) * (1 - 2 * bit))

    def parts_of(s, n):
        return plans[goes_line_first(n, len(bits))][s]

    def box(row, size, cols):
        at = pl.ds(row if isinstance(row, int) else pl.multiple_of(row, 16), size)
        first = cols[0] if isinstance(cols[0], int) else pl.multiple_of(cols[0], 128)
        return at, pl.ds(first, cols[1])

    def copy_to(d, src, dst, pair):
        pltpu.make_async_remote_copy(
            src_ref=src,
            dst_ref=dst,
            send_sem=pair[0],
            recv_sem=pair[1],
            device_id=peers[d],
            device_id_type=MESH,
        ).start()

    def pair_of(kind, s, slot):
        if kind == "reduce":
            return rs_send.at[s, slot], rs_recv.at[s, slot]
        return ag_send.at[s, slot], ag_recv.at[s, slot]

    def send_block(kind, s, n, slot):
        pair = pair_of(kind, s, slot)
        for keep, send, size, cols, sent_cols, at, at_cols, d in parts_of(s, n):
            if kind == "reduce":
                copy_to(
                    d, w.at[n, *box(send, size, sent_cols)], inbox[s].at[slot, *box(at, size, at_cols)], pair
                )
            else:
                own = w.at[n, *box(keep, size, cols)]
                copy_to(d, own, own, pair)

    def settle(like, pair):
        for sem in pair:
            pltpu.make_async_copy(like, like, sem).wait()

    def take_block(kind, s, n, slot):
        settle(inbox[s].at[slot if kind == "reduce" else 0], pair_of(kind, s, slot))
        if kind == "reduce":
            for keep, _, size, cols, _, at, at_cols, _ in parts_of(s, n):
                for i in range(0, size, 128):
                    step = min(size, 128)
                    mine = (n, *box(keep + i, step, cols))
                    got = inbox[s][slot, *box(at + i, step, at_cols)]
                    w[mine] = (w[mine].astype(F32) + got.astype(F32)).astype(BF16)

    sum_dirs = ["core", "x", *range(len(bits)), "y"]

    def sum_rows(s):
        return pl.ds(0, 8 if s + 1 < len(sum_dirs) else 16)

    def send_sums(s):
        src, dst = sums.at[sum_rows(s)], sums_in.at[s, sum_rows(s)]
        copy_to(sum_dirs[s], src, dst, (sum_send.at[s], sum_recv.at[s]))

    def take_sums(s):
        settle(sums_in.at[s, sum_rows(s)], (sum_send.at[s], sum_recv.at[s]))
        if s + 1 < len(sum_dirs):
            sums[0:8, :] = sums[0:8, :] + sums_in[s, 0:8, :]

    low[...] = hid[...].astype(BF16)

    def pieces_of(i):
        t = 1 - i
        base = i * 12
        work = {}

        def down(f):
            slope[t, f] = (nt(low[...], w[base + f]) * slope[t, f].astype(F32)).astype(BF16)
            w[base + f] = tn(gate[t, f], low[...]).astype(BF16)

        def feed(f):
            if f == 0:
                tr[...] = act2[t].T
                mid[...] = nt(slope[t, f], w[base + 4 + f])
            else:
                mid[...] += nt(slope[t, f], w[base + 4 + f])

        def up(f):
            w[base + 4 + f] = nn(tr[...], slope[t, f]).astype(BF16)

        def attended():
            dob[...] = nt(low[...], w[base + 8]).astype(BF16)

        def head_back(h):
            lanes = pl.ds(h * head, head)
            keys = kv[t, :, lanes]
            values = kv[t, :, pl.ds(BLOCK + h * head, head)]
            weight = prob[t, h]
            grad_out = dob[:, lanes]
            grad_weight = nt(values, grad_out)
            spread = weight.astype(F32) * grad_weight
            delta = jnp.sum(spread, 0, keepdims=True)
            ds = (spread - weight.astype(F32) * delta).astype(BF16)
            dv = nn(weight, grad_out)
            dk = nn(ds, qv[t, :, lanes]) * (head ** (-0.5))
            dq_t = tn(keys, ds) * (head ** (-0.5))
            dqkv[:, lanes] = dq_t.T.astype(BF16)
            dkv[:, lanes] = dk[:rows]
            dkv[:, pl.ds(BLOCK + h * head, head)] = dv[:rows]
            rim[:, lanes] = dk[rows:].astype(BF16)
            rim[:, pl.ds(BLOCK + h * head, head)] = dv[rows:].astype(BF16)

        copies = []

        def send_halo():
            copies.extend(
                halo_copies(
                    2 + t, rim, rin.at[t, pl.ds(halo, halo), :], rin.at[t, pl.ds(0, halo), :]
                )
            )
            for copy in copies:
                copy.start()

        def out():
            w[base + 8] = nn(att_t[t], low[...]).astype(BF16)

        def project(k):
            lanes = pl.ds(k * BLOCK, BLOCK)
            back = nt(dqkv[:, lanes], w[base + 9 + k])
            if k == 0:
                tr[...] = act1[t].T
                hid[...] = back
            else:
                hid[...] += back
            w[base + 9 + k] = nn(tr[...], dqkv[:, lanes]).astype(BF16)

        def whole_table():
            for copy in copies:
                copy.wait()
            dqkv[:, pl.ds(BLOCK, 2 * BLOCK)] = (dkv[...] + nn(sel_t[...], rin[t])).astype(BF16)

        for f in range(4):
            work[f"down{f}"] = functools.partial(down, f)
            work[f"feed{f}"] = functools.partial(feed, f)
            work[f"up{f}"] = functools.partial(up, f)
            work[f"head{f}"] = functools.partial(head_back, f)
        work["norm2"] = functools.partial(norm_back, t, 2, mid, xh2, rs2, hid, mid)
        work["attended"] = attended
        work["halo"] = send_halo
        work["out"] = out
        work["query"] = functools.partial(project, 0)
        work["table"] = whole_table
        work["key"] = functools.partial(project, 1)
        work["value"] = functools.partial(project, 2)
        work["norm1"] = functools.partial(norm_back, t, 0, hid, xh1, rs1, mid, hid)
        return work

    layers = [pieces_of(0), pieces_of(1)]
    for act, *rest in order:
        if act == "work":
            name, i = rest
            layers[i][name]()
        else:
            kind, s, n, slot = rest
            if kind == "sums":
                (send_sums if act == "send" else take_sums)(s)
            elif kind == "token":
                if act == "send":
                    told = token.at[s if isinstance(s, int) else len(bits) + "xyc".index(s[0])]
                    pl.semaphore_signal(told, inc=1, device_id=peers[s], device_id_type=MESH)
                else:
                    pl.semaphore_wait(told, 1)
            else:
                (send_block if act == "send" else take_block)(kind, s, n, slot)

    igrad_ref[0] = hid[...]
    far_sums = len(sum_dirs) - 1
    other = features(jnp.concatenate([sums_in[far_sums, 8:16, 0:128]] * (COND // 8), axis=0))
    for t in range(2):
        for i in range(4):
            row = pl.ds(t * 4 + i, 1)
            cond_grad_ref[t, i] = wide * sums[row, :] + other * sums_in[far_sums, row, :]


def widen(
    result_in, igrad_in, cond_in, w, result, igrad, cond, qkv, out, up, down, stage, sems, small
):
    copies = [
        pltpu.make_async_copy(src, dst, small.at[i])
        for i, (src, dst) in enumerate(
            ((result_in, result), (igrad_in, igrad), (cond_in, cond))
        )
    ]
    for copy in copies:
        copy.start()
    slots = stage.shape[0]
    pending = [None] * slots
    for n in range(24):
        t, k, slot = 1 - n // 12, n % 12, n % slots
        if pending[slot] is not None:
            pending[slot].wait()
        stage[slot] = w[n].astype(F32)
        if k < 4:
            dst = down.at[t, pl.ds(k * BLOCK, BLOCK), :]
        elif k < 8:
            dst = up.at[t, :, pl.ds((k - 4) * BLOCK, BLOCK)]
        elif k < 9:
            dst = out.at[t]
        else:
            dst = qkv.at[t, :, pl.ds((k - 9) * BLOCK, BLOCK)]
        pending[slot] = pltpu.make_async_copy(stage.at[slot], dst, sems.at[slot])
        pending[slot].start()
    for copy in pending + copies:
        copy.wait()


def solution(mesh):
    patches = mesh.shape["patch"]

    def shards(nodes, noise, sizes, send, nbr, qkv, out, up, down, cond_w, cot):
        rows, width = nodes.shape[1:]
        halo2 = send.shape[0]
        halo = halo2 // 2
        table = rows + halo2
        freq = np.tile(2.0 ** (np.arange(COND) % (COND // 2) / 4.0), (128, 1)).T.astype(np.float32)
        vmem = pl.BlockSpec(memory_space=pltpu.VMEM)
        smem = pl.BlockSpec(memory_space=pltpu.SMEM)
        hbm = pl.BlockSpec(memory_space=pl.ANY)
        line_bits = (patches // 4).bit_length() - 1
        order = schedule(line_bits, SLOTS)
        stages = 3 + line_bits
        used = [1 + max(v[4] for v in order if v[:3] == ("send", "reduce", s)) for s in range(stages)]
        sems = [1 + max(v[4] for v in order if v[:3] == ("send", "gather", s)) for s in range(stages - 1)]
        boxes = [list(parts) for parts in exchanges(0, 0, 0, [0] * line_bits, False)]
        boxes = [
            (sum(p[2] * p[3][1] for p in parts) // min(BLOCK, parts[0][6][1] * len(parts)), min(BLOCK, parts[0][6][1] * len(parts)))
            for parts in boxes
        ]
        held = pl.pallas_call(
            functools.partial(mega, patches, order),
            out_shape=(
                pltpu.VMEM((1, rows, width), BF16),
                pltpu.VMEM((1, rows, width), F32),
                pltpu.VMEM(cond_w.shape, F32),
                pltpu.VMEM((24, BLOCK, BLOCK), BF16),
            ),
            in_specs=[smem, smem, vmem, vmem, vmem, vmem] + [hbm] * 6,
            out_specs=(vmem,) * 4,
            scratch_shapes=[
                pltpu.VMEM((table, rows), F32),
                pltpu.VMEM((halo2, rows), BF16),
                pltpu.VMEM((rows, halo2), BF16),
                pltpu.VMEM((8, 1, width), F32),
                pltpu.VMEM((rows, width), F32),
                pltpu.VMEM((rows, width), F32),
                pltpu.VMEM((2, rows, width), F32),
                pltpu.VMEM((2, rows, width), F32),
                pltpu.VMEM((2, rows, 1), F32),
                pltpu.VMEM((2, rows, 1), F32),
                pltpu.VMEM((2, rows, width), BF16),
                pltpu.VMEM((2, rows, width), BF16),
                pltpu.VMEM((rows, width), BF16),
                pltpu.VMEM((width, rows), BF16),
                pltpu.VMEM((2, rows, width), BF16),
                pltpu.VMEM((2, table, 2 * width), BF16),
                pltpu.VMEM((2, HEADS, table, rows), BF16),
                pltpu.VMEM((2, width, rows), BF16),
                pltpu.VMEM((2, 4, rows, BLOCK), BF16),
                pltpu.VMEM((2, 4, rows, BLOCK), BF16),
                pltpu.VMEM((rows, width), BF16),
                pltpu.VMEM((rows, 2 * width), F32),
                pltpu.VMEM((rows, 3 * width), BF16),
                pltpu.VMEM((halo2, 2 * width), BF16),
                pltpu.VMEM((2, halo2, 2 * width), BF16),
                pltpu.VMEM((rows, width), BF16),
                pltpu.VMEM((rows, width), BF16),
                pltpu.VMEM((16, width), F32),
                pltpu.VMEM((8, rows), F32),
                pltpu.VMEM((stages, 16, width), F32),
                pltpu.SemaphoreType.DMA((3, 12)),
                pltpu.SemaphoreType.DMA((4, 2)),
                pltpu.SemaphoreType.DMA((4, 2)),
                pltpu.SemaphoreType.DMA((stages, max(used))),
                pltpu.SemaphoreType.DMA((stages, max(used))),
                pltpu.SemaphoreType.DMA((stages - 1, max(sems))),
                pltpu.SemaphoreType.DMA((stages - 1, max(sems))),
                pltpu.SemaphoreType.DMA((stages,)),
                pltpu.SemaphoreType.DMA((stages,)),
                pltpu.SemaphoreType.REGULAR((stages,)),
                *(pltpu.VMEM((count, *shape), BF16) for count, shape in zip(used, boxes)),
            ],
            compiler_params=pltpu.CompilerParams(
                collective_id=0, has_side_effects=True, vmem_limit_bytes=49 * 2**20
            ),
        )(noise, sizes, send.reshape(1, -1), nbr, cond_w, freq, nodes, qkv, out, up, down, cot)
        held = [pltpu.with_memory_space_constraint(v, pltpu.VMEM) for v in held]
        result, igrad, cond_grad, *grads = pl.pallas_call(
            widen,
            out_shape=(
                jax.ShapeDtypeStruct((1, rows, width), BF16),
                jax.ShapeDtypeStruct((1, rows, width), F32),
                jax.ShapeDtypeStruct(cond_w.shape, F32),
                *(jax.ShapeDtypeStruct(v.shape, F32) for v in (qkv, out, up, down)),
            ),
            in_specs=[vmem] * 4,
            out_specs=(hbm,) * 7,
            scratch_shapes=[
                pltpu.VMEM((8, BLOCK, BLOCK), F32),
                pltpu.SemaphoreType.DMA((8,)),
                pltpu.SemaphoreType.DMA((3,)),
            ],
            compiler_params=pltpu.CompilerParams(vmem_limit_bytes=32 * 2**20),
        )(*held)
        return (result, igrad, *grads, cond_grad)

    placed = (
        P("noise", "patch", None),
        P("noise"),
        P("patch"),
        P("patch"),
        P(None, "patch"),
        P(),
        P(),
        P(),
        P(),
        P(),
        P("noise", "patch", None),
    )
    return jax.shard_map(
        shards,
        mesh=mesh,
        in_specs=placed,
        out_specs=(P("noise", "patch", None), P("noise", "patch", None), P(), P(), P(), P(), P()),
        check_vma=False,
    )
```

```python
import functools

import jax
import jax.numpy as jnp
import numpy as np
from jax import lax
from jax.experimental import pallas as pl
from jax.experimental.pallas import tpu as pltpu
from jax.sharding import PartitionSpec as P

HEADS = 4
COND = 32
SLOTS = 16
EPSILON = 1e-05
LOG2E = 1.4426950408889634
MESH = pl.DeviceIdType.MESH
F32 = jnp.float32
BF16 = jnp.bfloat16
BLOCK = 512


WHOLE, LEFT, RIGHT = (0, BLOCK), (0, BLOCK // 2), (BLOCK // 2, BLOCK // 2)


def square(row, size, x, y, last):
    one, two = size // 2, size // 4
    first = [(row + x * one, row + (1 - x) * one, one, LEFT, LEFT, 0, LEFT, "x")]
    second = []
    for i in range(2):
        at = row + i * one
        first.append((at + y * two, at + (1 - y) * two, two, RIGHT, RIGHT, i * two, RIGHT, "y"))
        if last:
            second.append((at + y * two, at + y * two, two, RIGHT, RIGHT, i * two, RIGHT, "x"))
    mine = row + x * one
    kept = mine + y * two
    if last:
        second.append((mine, mine, one, LEFT, LEFT, 0, LEFT, "y"))
    else:
        second.append((kept, mine + (1 - y) * two, two, LEFT, LEFT, 0, LEFT, "y"))
        other = row + (1 - x) * one + y * two
        second.append((kept, other, two, RIGHT, RIGHT, 0, RIGHT, "x"))
    return kept, two, first, second


def along_line(row, size, cols, bit, b, last):
    if last:
        return (row, size, cols), [(row, row, size, cols, cols, 0, (0, cols[1]), b)]
    if size >= 32:
        size //= 2
        keep, send = row + bit * size, row + (1 - bit) * size
        return (keep, size, cols), [(keep, send, size, cols, cols, 0, (0, cols[1]), b)]
    first, width = cols[0], cols[1] // 2
    keep, send = (first + bit * width, width), (first + (1 - bit) * width, width)
    return (row, size, keep), [(row, row, size, keep, send, 0, (0, width), b)]


def exchanges(core, x, y, bits, line_first):
    half = BLOCK // 2
    row, size, cols = core * half, half, WHOLE
    out = [[(row, (1 - core) * half, half, WHOLE, WHOLE, 0, WHOLE, "core")]]
    if not line_first:
        row, size, first, second = square(row, size, x, y, False)
        out += [first, second]
    for b, bit in enumerate(bits):
        last = not line_first and b == len(bits) - 1
        (row, size, cols), parts = along_line(row, size, cols, bit, b, last)
        out.append(parts)
    if line_first:
        row, size, first, second = square(row, size, x, y, True)
        out += [first, second]
    return out


LINE_FIRST = (4, 13, 16, 21)


def goes_line_first(n, line_bits):
    return line_bits == 2 and n in LINE_FIRST


MADE = {
    **{f"down{f}": f for f in range(4)},
    **{f"up{f}": 4 + f for f in range(4)},
    **{"out": 8, "query": 9, "key": 10, "value": 11},
}
LAYER_PIECES = (
    (
        "down0", "down1", "feed0", "down2", "feed1", "down3", "feed2", "feed3", "up0", "norm2", "attended",
        "up3", "head0", "up1", "head1", "halo0", "head2", "head3", "halo1", "up2", "out", "query", "table",
        "key", "value", "norm1",
    ),
    (
        "down0", "down1", "down2", "feed0", "feed1", "feed2", "down3", "feed3", "norm2", "up2", "attended",
        "head0", "up1", "head1", "halo0", "up0", "head2", "head3", "up3", "halo1", "query", "out", "table",
        "key", "value", "norm1",
    ),
)

REDUCE_LAGS = ((1, 3, 2, 3, 4), (1, 4, 4, 3, 2))
GATHER_LAGS = ((3, 3, 7, 3), (2, 4, 7, 5))
GATHER_WAIT = (1, 1)
SUMS_LAG = 3


def schedule(line_bits, slots):
    tables = [exchanges(0, 0, 0, [0] * line_bits, f) for f in (False, True)]
    stages = 3 + line_bits
    sum_dirs = ["core", "x", *range(line_bits), "y"]

    def dirs_of(kind, s, n):
        if kind == "sums":
            return {sum_dirs[s]}
        return {p[7] for p in tables[goes_line_first(n, line_bits)][s]}

    order, sent, seen = [], [], set()
    reduced = {}
    places = {}

    def told(since, dirs):
        return all(
            any(at > since and d in ds and key in seen for at, ds, key in sent) for d in dirs
        )

    def find_slot(kind, s, dirs):
        for slot in range(slots):
            since = places.get((kind, s, slot), -1)
            if since == -1 or (since is not None and told(since, dirs)):
                return slot
        return None

    def lag(kind, s, n):
        if kind == "sums":
            return SUMS_LAG
        lags = (REDUCE_LAGS if kind == "reduce" else GATHER_LAGS)[goes_line_first(n, line_bits)]
        if kind == "reduce":
            return lags[min(s, len(lags) - 1)]
        return lags[max(0, len(lags) - 1 - s)]

    flying, waiting = [], []

    def start_due(turn):
        for item in sorted(v for v in waiting if v[0] <= turn):
            _, kind, s, n = item
            dirs = dirs_of(kind, s, n)
            if kind == "gather" and not told(reduced[s, n], dirs):
                continue
            slot = 0 if kind == "sums" else find_slot(kind, s, dirs)
            if slot is None:
                continue
            waiting.remove(item)
            order.append(("send", kind, s, n, slot))
            places[kind, s, slot] = None
            sent.append((len(order), dirs, (kind, s, n)))
            flying.append((turn + lag(kind, s, n), kind, s, n, slot))

    def take_turn(turn):
        due = [v for v in flying if v[0] <= turn]
        rank = {"gather": 0, "sums": 1, "reduce": 2}
        due.sort(key=lambda v: (rank[v[1]], v[2] if v[1] == "gather" else -v[2], v[3]))
        for item in due:
            flying.remove(item)
            _, kind, s, n, slot = item
            order.append(("take", kind, s, n, slot))
            seen.add((kind, s, n))
            places[kind, s, slot] = len(order)
            if kind == "reduce":
                reduced[s, n] = len(order)
                if s + 1 < stages:
                    waiting.append((turn, kind, s + 1, n))
                else:
                    wait = GATHER_WAIT[goes_line_first(n, line_bits)]
                    waiting.append((turn + wait, "gather", s - 1, n))
            elif kind == "gather" and s > 0:
                waiting.append((turn, kind, s - 1, n))
            elif kind == "sums" and s + 1 < len(sum_dirs):
                waiting.append((turn, kind, s + 1, n))
            start_due(turn)
        start_due(turn)

    turn = 0
    for i in range(2):
        for name in LAYER_PIECES[i]:
            order.append(("work", name, i))
            if name in MADE:
                waiting.append((turn, "reduce", 0, i * 12 + MADE[name]))
                take_turn(turn)
                turn += 1
    waiting.append((turn, "sums", 0, 0))
    while flying or waiting:
        before = len(order)
        take_turn(turn)
        turn += 1
        if len(order) == before and not flying:
            for d in dirs_of(*waiting[0][1:]):
                order += [("send", "token", d, 0, 0), ("take", "token", d, 0, 0)]
                sent.append((len(order), {d}, ("token", len(order))))
                seen.add(("token", len(order)))
    return order


def nn(a, b):
    return lax.dot_general(a, b, (((1,), (0,)), ((), ())), preferred_element_type=F32)


def nt(a, b):
    return lax.dot_general(a, b, (((1,), (1,)), ((), ())), preferred_element_type=F32)


def tn(a, b):
    return lax.dot_general(a, b, (((0,), (0,)), ((), ())), preferred_element_type=F32)


def mega(
    patches,
    order,
    noise_ref,
    sizes_ref,
    send_ref,
    nbr_ref,
    cond_w_ref,
    freq_ref,
    nodes_hbm,
    qkv_hbm,
    out_hbm,
    up_hbm,
    down_hbm,
    cot_hbm,
    result_ref,
    igrad_ref,
    cond_grad_ref,
    w,
    logc,
    sel,
    sel_t,
    cond,
    hid,
    mid,
    xh1,
    xh2,
    rs1,
    rs2,
    act1,
    act2,
    low,
    tr,
    qv,
    kv,
    prob,
    att_t,
    gate,
    slope,
    dob,
    dkv,
    dqkv,
    rim,
    rin,
    node_in,
    cot_in,
    sums,
    stat,
    sums_in,
    load_sem,
    halo_send,
    halo_recv,
    rs_send,
    rs_recv,
    ag_send,
    ag_recv,
    sum_send,
    sum_recv,
    token,
    *inbox,
):
    rows = hid.shape[0]
    table = kv.shape[1]
    halo = rim.shape[0] // 2
    my_noise = lax.axis_index("noise")
    me = lax.axis_index("patch")
    before = (my_noise, lax.rem(me + patches - 1, patches))
    after = (my_noise, lax.rem(me + 1, patches))

    def place(t, k, down, up, out, qkv):
        if k < 4:
            return down.at[t, pl.ds(k * BLOCK, BLOCK), :]
        if k < 8:
            return up.at[t, :, pl.ds((k - 4) * BLOCK, BLOCK)]
        if k < 9:
            return out.at[t]
        return qkv.at[t, :, pl.ds((k - 9) * BLOCK, BLOCK)]

    def load(t, k):
        src = place(t, k, down_hbm, up_hbm, out_hbm, qkv_hbm)
        return pltpu.make_async_copy(src, w.at[(1 - t) * 12 + k], load_sem.at[t])

    node_copy = pltpu.make_async_copy(nodes_hbm.at[0], node_in, load_sem.at[2])
    cot_copy = pltpu.make_async_copy(cot_hbm.at[0], cot_in, load_sem.at[3])
    node_copy.start()
    for t in range(2):
        for k in (9, 10, 11, 8, 4, 0, 5, 1, 6, 2, 7, 3):
            load(t, k).start()
    cot_copy.start()

    core = lax.rem(me, 2)
    x = lax.rem(me // 2, 2)
    y = my_noise
    z = me // 4
    line = patches // 4
    core_peer = (my_noise, me + 1 - 2 * core)
    x_peer = (my_noise, me + 2 - 4 * x)
    y_peer = (1 - my_noise, me)

    barrier = pltpu.get_barrier_semaphore()
    greeted = [before, after, core_peer, x_peer, y_peer]
    for b in range(line.bit_length() - 1):
        bit = lax.rem(z // (1 << b), 2)
        greeted.append((my_noise, me + 4 * (1 << b) * (1 - 2 * bit)))
    for other in greeted:
        pl.semaphore_signal(barrier, inc=1, device_id=other, device_id_type=MESH)

    step_rows = 64

    def count(i, _):
        base = i * step_rows
        ids = lax.broadcasted_iota(jnp.int32, (step_rows, rows), 0) + base
        total = jnp.zeros((step_rows, rows), F32)
        for j in range(nbr_ref.shape[0]):
            total = total + jnp.where(nbr_ref[j : j + 1, :] == ids, 1.0, 0.0)
        logc[pl.ds(base, step_rows), :] = jnp.where(total > 0.0, jnp.log(total) * LOG2E, -1e30)
        return 0

    lax.fori_loop(0, table // step_rows, count, 0)
    picked = jnp.where(
        lax.broadcasted_iota(jnp.int32, (rows, 2 * halo), 0) == send_ref[...], 1.0, 0.0
    )
    sel_t[...] = picked.astype(BF16)
    sel[...] = picked.T.astype(BF16)

    def features(noise):
        phase = jnp.log(noise) * freq_ref[...]
        is_sin = lax.broadcasted_iota(jnp.int32, (COND, 128), 0) < COND // 2
        feats = jnp.where(is_sin, jnp.sin(phase), jnp.cos(phase))
        return jnp.concatenate([feats] * (hid.shape[1] // 128), axis=1)

    wide = features(jnp.broadcast_to(noise_ref[...], (COND, 128)))
    sums[8:16, :] = jnp.broadcast_to(noise_ref[...], (8, hid.shape[1]))
    for t in range(2):
        for i in range(4):
            cond[t * 4 + i] = jnp.sum(cond_w_ref[t, i].astype(F32) * wide, 0, keepdims=True)

    node_copy.wait()
    hid[...] = node_in[...].astype(F32)
    pl.semaphore_wait(barrier, len(greeted))

    head = hid.shape[1] // HEADS
    unit = LOG2E * head ** (-0.5)
    ln_rows = 64

    def norm(value_ref, t, first, normed_ref, inv_ref, out_ref):
        def body(i, _):
            at = pl.ds(i * ln_rows, ln_rows)
            value = value_ref[at, :]
            centred = value - jnp.mean(value, -1, keepdims=True)
            inv = lax.rsqrt(jnp.mean(centred * centred, -1, keepdims=True) + EPSILON)
            normed = centred * inv
            normed_ref[t, at, :] = normed
            inv_ref[t, at, :] = inv
            out_ref[t, at, :] = (
                normed * (1.0 + cond[t * 4 + first]) + cond[t * 4 + first + 1]
            ).astype(BF16)
            return 0

        lax.fori_loop(0, rows // ln_rows, body, 0, unroll=4)

    def halo_copies(stage, part, src, dst, to_before, to_after):
        cols = pl.ds(part * BLOCK, BLOCK)
        return [
            pltpu.make_async_remote_copy(
                src_ref=src.at[pl.ds(i * halo, halo), cols],
                dst_ref=dst.at[pl.ds(row, halo), cols],
                send_sem=halo_send.at[stage * 2 + part, i],
                recv_sem=halo_recv.at[stage * 2 + part, i],
                device_id=other,
                device_id_type=MESH,
            )
            for i, (row, other) in enumerate(((to_before, before), (to_after, after)))
        ]

    def forward(t, _):
        base = (1 - t) * 12
        layer = w.at[pl.ds(base, 12)]
        pltpu.make_async_copy(layer, layer, load_sem.at[t]).wait()
        norm(hid, t, 0, xh1, rs1, act1)
        a = act1[t]
        copies = []
        for part in range(2):
            cols = pl.ds(part * BLOCK, BLOCK)
            kv[t, pl.ds(0, rows), cols] = nn(a, w[base + 10 + part]).astype(BF16)
            rim[:, cols] = nn(sel[...], kv[t, pl.ds(0, rows), cols]).astype(BF16)
            copies.append(halo_copies(t, part, rim, kv.at[t], rows + halo, rows))
            for copy in copies[part]:
                copy.start()
        qv[t] = nn(a, w[base + 9]).astype(BF16)
        own, far = pl.ds(0, rows), pl.ds(rows, table - rows)
        for h in range(HEADS):
            lanes = pl.ds(h * head, head)
            for c in range(2):
                cols = pl.ds(c * 256, 256)
                score = nt(kv[t, own, lanes], qv[t, cols, lanes]) * unit + logc[own, cols]
                top = jnp.max(score, 0, keepdims=True)
                part = jnp.exp2(score - top)
                prob[t, h, own, cols] = part.astype(BF16)
                stat[2 * h : 2 * h + 1, cols] = top
                stat[2 * h + 1 : 2 * h + 2, cols] = jnp.sum(part, 0, keepdims=True)
        for copy in copies[0]:
            copy.wait()
        for h in range(HEADS):
            lanes = pl.ds(h * head, head)
            score = nt(kv[t, far, lanes], qv[t, :, lanes]) * unit + logc[far, :]
            near_top = stat[2 * h : 2 * h + 1, :]
            top = jnp.maximum(near_top, jnp.max(score, 0, keepdims=True))
            part = jnp.exp2(score - top)
            scale = jnp.exp2(near_top - top)
            inv = 1.0 / (stat[2 * h + 1 : 2 * h + 2, :] * scale + jnp.sum(part, 0, keepdims=True))
            prob[t, h, far, :] = (part * inv).astype(BF16)
            prob[t, h, own, :] = (prob[t, h, own, :].astype(F32) * (scale * inv)).astype(BF16)
        for copy in copies[1]:
            copy.wait()
        for h in range(HEADS):
            lanes = pl.ds(h * head, head)
            values = kv[t, :, pl.ds(BLOCK + h * head, head)]
            att_t[t, lanes, :] = tn(values, prob[t, h]).astype(BF16)
        mid[...] = hid[...] + tn(att_t[t], w[base + 8])
        norm(mid, t, 2, xh2, rs2, act2)
        for f in range(4):
            u = nn(act2[t], w[base + 4 + f])
            sig = 0.5 * jnp.tanh(0.5 * u) + 0.5
            g = u * sig
            gate[t, f] = g.astype(BF16)
            slope[t, f] = (sig + g * (1.0 - sig)).astype(BF16)
            if f == 0:
                hid[...] = mid[...] + nn(gate[t, f], w[base + f])
            else:
                hid[...] += nn(gate[t, f], w[base + f])
        return 0

    lax.fori_loop(0, 2, forward, 0)

    cot_copy.wait()

    def turn(i, _):
        at = pl.ds(i * ln_rows, ln_rows)
        ids = lax.broadcasted_iota(jnp.int32, (ln_rows, hid.shape[1]), 0) + i * ln_rows
        live = ids < sizes_ref[...]
        result_ref[0, at, :] = jnp.where(live, hid[at, :], 0.0).astype(BF16)
        hid[at, :] = jnp.where(live, cot_in[at, :].astype(F32), 0.0)
        return 0

    lax.fori_loop(0, rows // ln_rows, turn, 0)

    def norm_back(t, first, grad_ref, normed_ref, inv_ref, add_ref, out_ref):
        def body(i, carry):
            scale_sum, shift_sum = carry
            at = pl.ds(i * ln_rows, ln_rows)
            grad = grad_ref[at, :]
            normed = normed_ref[t, at, :]
            back = grad * normed
            scale_sum = scale_sum + jnp.sum(back.reshape(-1, 8, hid.shape[1]), 0)
            shift_sum = shift_sum + jnp.sum(grad.reshape(-1, 8, hid.shape[1]), 0)
            scaled = grad * (1.0 + cond[t * 4 + first])
            one = jnp.mean(scaled, -1, keepdims=True)
            two = jnp.mean(scaled * normed, -1, keepdims=True)
            out = add_ref[at, :] + inv_ref[t, at, :] * (scaled - one - normed * two)
            out_ref[at, :] = out
            low[at, :] = out.astype(BF16)
            return scale_sum, shift_sum

        zero = jnp.zeros((8, hid.shape[1]), F32)
        scale_sum, shift_sum = lax.fori_loop(0, rows // ln_rows, body, (zero, zero), unroll=4)
        sums[pl.ds(t * 4 + first, 1), :] = jnp.sum(scale_sum, 0, keepdims=True)
        sums[pl.ds(t * 4 + first + 1, 1), :] = jnp.sum(shift_sum, 0, keepdims=True)

    bits = [lax.rem(z // (1 << b), 2) for b in range(line.bit_length() - 1)]
    stages = 3 + len(bits)
    plans = [exchanges(core, x, y, bits, f) for f in (False, True)]
    peers = {"core": core_peer, "x": x_peer, "y": y_peer}
    for b, bit in enumerate(bits):
        peers[b] = (my_noise, me + 4 * (1 << b) * (1 - 2 * bit))

    def parts_of(s, n):
        return plans[goes_line_first(n, len(bits))][s]

    def box(row, size, cols):
        at = pl.ds(row if isinstance(row, int) else pl.multiple_of(row, 16), size)
        first = cols[0] if isinstance(cols[0], int) else pl.multiple_of(cols[0], 128)
        return at, pl.ds(first, cols[1])

    def copy_to(d, src, dst, pair):
        pltpu.make_async_remote_copy(
            src_ref=src,
            dst_ref=dst,
            send_sem=pair[0],
            recv_sem=pair[1],
            device_id=peers[d],
            device_id_type=MESH,
        ).start()

    def pair_of(kind, s, slot):
        if kind == "reduce":
            return rs_send.at[s, slot], rs_recv.at[s, slot]
        return ag_send.at[s, slot], ag_recv.at[s, slot]

    def send_block(kind, s, n, slot):
        pair = pair_of(kind, s, slot)
        for keep, send, size, cols, sent_cols, at, at_cols, d in parts_of(s, n):
            if kind == "reduce":
                copy_to(
                    d, w.at[n, *box(send, size, sent_cols)], inbox[s].at[slot, *box(at, size, at_cols)], pair
                )
            else:
                own = w.at[n, *box(keep, size, cols)]
                copy_to(d, own, own, pair)

    def settle(like, pair):
        for sem in pair:
            pltpu.make_async_copy(like, like, sem).wait()

    def take_block(kind, s, n, slot):
        settle(inbox[s].at[slot if kind == "reduce" else 0], pair_of(kind, s, slot))
        if kind == "reduce":
            for keep, _, size, cols, _, at, at_cols, _ in parts_of(s, n):
                step = min(size, 32)

                def add(i, _, keep=keep, cols=cols, at=at, at_cols=at_cols, step=step):
                    mine = (n, *box(keep + i * step, step, cols))
                    got = inbox[s][slot, *box(at + i * step, step, at_cols)]
                    w[mine] = (w[mine].astype(F32) + got.astype(F32)).astype(BF16)
                    return 0

                lax.fori_loop(0, size // step, add, 0)

    sum_dirs = ["core", "x", *range(len(bits)), "y"]

    def sum_rows(s):
        return pl.ds(0, 8 if s + 1 < len(sum_dirs) else 16)

    def send_sums(s):
        src, dst = sums.at[sum_rows(s)], sums_in.at[s, sum_rows(s)]
        copy_to(sum_dirs[s], src, dst, (sum_send.at[s], sum_recv.at[s]))

    def take_sums(s):
        settle(sums_in.at[s, sum_rows(s)], (sum_send.at[s], sum_recv.at[s]))
        if s + 1 < len(sum_dirs):
            sums[0:8, :] = sums[0:8, :] + sums_in[s, 0:8, :]

    low[...] = hid[...].astype(BF16)

    def pieces_of(i):
        t = 1 - i
        base = i * 12
        work = {}

        def down(f):
            slope[t, f] = (nt(low[...], w[base + f]) * slope[t, f].astype(F32)).astype(BF16)
            w[base + f] = tn(gate[t, f], low[...]).astype(BF16)

        def feed(f):
            if f == 0:
                tr[...] = act2[t].T
                mid[...] = nt(slope[t, f], w[base + 4 + f])
            else:
                mid[...] += nt(slope[t, f], w[base + 4 + f])

        def up(f):
            w[base + 4 + f] = nn(tr[...], slope[t, f]).astype(BF16)

        def attended():
            dob[...] = nt(low[...], w[base + 8]).astype(BF16)

        def head_back(h):
            lanes = pl.ds(h * head, head)
            keys = kv[t, :, lanes]
            values = kv[t, :, pl.ds(BLOCK + h * head, head)]
            weight = prob[t, h]
            grad_out = dob[:, lanes]
            grad_weight = nt(values, grad_out)
            spread = weight.astype(F32) * grad_weight
            delta = jnp.sum(spread, 0, keepdims=True)
            ds = (spread - weight.astype(F32) * delta).astype(BF16)
            dv = nn(weight, grad_out)
            dk = nn(ds, qv[t, :, lanes]) * (head ** (-0.5))
            dq_t = tn(keys, ds) * (head ** (-0.5))
            dqkv[:, lanes] = dq_t.T.astype(BF16)
            dkv[:, lanes] = dk[:rows]
            dkv[:, pl.ds(BLOCK + h * head, head)] = dv[:rows]
            first = (h // 2) * BLOCK + (h % 2) * head
            rim[:, pl.ds(first, head)] = dk[rows:].astype(BF16)
            rim[:, pl.ds(first + BLOCK // 2, head)] = dv[rows:].astype(BF16)

        copies = []

        def send_halo(part):
            copies.extend(halo_copies(2 + t, part, rim, rin.at[t], halo, 0))
            for copy in copies[-2:]:
                copy.start()

        def out():
            w[base + 8] = nn(att_t[t], low[...]).astype(BF16)

        def project(k):
            lanes = pl.ds(k * BLOCK, BLOCK)
            back = nt(dqkv[:, lanes], w[base + 9 + k])
            if k == 0:
                tr[...] = act1[t].T
                hid[...] = back
            else:
                hid[...] += back
            w[base + 9 + k] = nn(tr[...], dqkv[:, lanes]).astype(BF16)

        def whole_table():
            for copy in copies:
                copy.wait()
            for part in range(2):
                back = nn(sel_t[...], rin[t, :, pl.ds(part * BLOCK, BLOCK)])
                for i in range(2):
                    half = BLOCK // 2
                    first = i * BLOCK + part * half
                    total = dkv[:, pl.ds(first, half)] + back[:, i * half : (i + 1) * half]
                    dqkv[:, pl.ds(BLOCK + first, half)] = total.astype(BF16)

        for f in range(4):
            work[f"down{f}"] = functools.partial(down, f)
            work[f"feed{f}"] = functools.partial(feed, f)
            work[f"up{f}"] = functools.partial(up, f)
            work[f"head{f}"] = functools.partial(head_back, f)
        work["norm2"] = functools.partial(norm_back, t, 2, mid, xh2, rs2, hid, mid)
        work["attended"] = attended
        work["halo0"] = functools.partial(send_halo, 0)
        work["halo1"] = functools.partial(send_halo, 1)
        work["out"] = out
        work["query"] = functools.partial(project, 0)
        work["table"] = whole_table
        work["key"] = functools.partial(project, 1)
        work["value"] = functools.partial(project, 2)
        work["norm1"] = functools.partial(norm_back, t, 0, hid, xh1, rs1, mid, hid)
        return work

    layers = [pieces_of(0), pieces_of(1)]
    for act, *rest in order:
        if act == "work":
            name, i = rest
            layers[i][name]()
        else:
            kind, s, n, slot = rest
            if kind == "sums":
                (send_sums if act == "send" else take_sums)(s)
            elif kind == "token":
                if act == "send":
                    told = token.at[s if isinstance(s, int) else len(bits) + "xyc".index(s[0])]
                    pl.semaphore_signal(told, inc=1, device_id=peers[s], device_id_type=MESH)
                else:
                    pl.semaphore_wait(told, 1)
            else:
                (send_block if act == "send" else take_block)(kind, s, n, slot)

    igrad_ref[0] = hid[...]
    far_sums = len(sum_dirs) - 1
    other = features(jnp.concatenate([sums_in[far_sums, 8:16, 0:128]] * (COND // 8), axis=0))
    for t in range(2):
        for i in range(4):
            row = pl.ds(t * 4 + i, 1)
            cond_grad_ref[t, i] = wide * sums[row, :] + other * sums_in[far_sums, row, :]


def widen(
    result_in, igrad_in, cond_in, w, result, igrad, cond, qkv, out, up, down, stage, sems, small
):
    copies = [
        pltpu.make_async_copy(src, dst, small.at[i])
        for i, (src, dst) in enumerate(
            ((result_in, result), (igrad_in, igrad), (cond_in, cond))
        )
    ]
    for copy in copies:
        copy.start()
    slots = stage.shape[0]

    def leave(n, _):
        slot, k, t = lax.rem(n, slots), lax.rem(n, 12), 1 - n // 12

        @pl.when(n >= slots)
        def _():
            pltpu.make_async_copy(stage.at[slot], out.at[0], sems.at[slot]).wait()

        def convert(i, _):
            at = pl.ds(pl.multiple_of(i * 128, 128), 128)
            stage[slot, at, :] = w[n, at, :].astype(F32)
            return 0

        lax.fori_loop(0, BLOCK // 128, convert, 0)
        for first, last in ((0, 4), (4, 8), (8, 9), (9, 12)):

            @pl.when((k >= first) & (k < last))
            def _():
                at = pl.ds(pl.multiple_of((k - first) * BLOCK, BLOCK), BLOCK)
                dst = {
                    0: down.at[t, at, :],
                    4: up.at[t, :, at],
                    8: out.at[t],
                    9: qkv.at[t, :, at],
                }[first]
                pltpu.make_async_copy(stage.at[slot], dst, sems.at[slot]).start()

        return 0

    lax.fori_loop(0, 24, leave, 0)
    for slot in range(slots):
        pltpu.make_async_copy(stage.at[slot], out.at[0], sems.at[slot]).wait()
    for copy in copies:
        copy.wait()


def solution(mesh):
    patches = mesh.shape["patch"]

    def shards(nodes, noise, sizes, send, nbr, qkv, out, up, down, cond_w, cot):
        rows, width = nodes.shape[1:]
        halo2 = send.shape[0]
        halo = halo2 // 2
        table = rows + halo2
        freq = np.tile(2.0 ** (np.arange(COND) % (COND // 2) / 4.0), (128, 1)).T.astype(np.float32)
        vmem = pl.BlockSpec(memory_space=pltpu.VMEM)
        hbm = pl.BlockSpec(memory_space=pl.ANY)
        line_bits = (patches // 4).bit_length() - 1
        order = schedule(line_bits, SLOTS)
        stages = 3 + line_bits
        used = [1 + max(v[4] for v in order if v[:3] == ("send", "reduce", s)) for s in range(stages)]
        sems = [1 + max(v[4] for v in order if v[:3] == ("send", "gather", s)) for s in range(stages - 1)]
        boxes = [list(parts) for parts in exchanges(0, 0, 0, [0] * line_bits, False)]
        boxes = [
            (sum(p[2] * p[3][1] for p in parts) // min(BLOCK, parts[0][6][1] * len(parts)), min(BLOCK, parts[0][6][1] * len(parts)))
            for parts in boxes
        ]
        held = pl.pallas_call(
            functools.partial(mega, patches, order),
            out_shape=(
                pltpu.VMEM((1, rows, width), BF16),
                pltpu.VMEM((1, rows, width), F32),
                pltpu.VMEM(cond_w.shape, F32),
                pltpu.VMEM((24, BLOCK, BLOCK), BF16),
            ),
            in_specs=[vmem] * 6 + [hbm] * 6,
            out_specs=(vmem,) * 4,
            scratch_shapes=[
                pltpu.VMEM((table, rows), F32),
                pltpu.VMEM((halo2, rows), BF16),
                pltpu.VMEM((rows, halo2), BF16),
                pltpu.VMEM((8, 1, width), F32),
                pltpu.VMEM((rows, width), F32),
                pltpu.VMEM((rows, width), F32),
                pltpu.VMEM((2, rows, width), F32),
                pltpu.VMEM((2, rows, width), F32),
                pltpu.VMEM((2, rows, 1), F32),
                pltpu.VMEM((2, rows, 1), F32),
                pltpu.VMEM((2, rows, width), BF16),
                pltpu.VMEM((2, rows, width), BF16),
                pltpu.VMEM((rows, width), BF16),
                pltpu.VMEM((width, rows), BF16),
                pltpu.VMEM((2, rows, width), BF16),
                pltpu.VMEM((2, table, 2 * width), BF16),
                pltpu.VMEM((2, HEADS, table, rows), BF16),
                pltpu.VMEM((2, width, rows), BF16),
                pltpu.VMEM((2, 4, rows, BLOCK), BF16),
                pltpu.VMEM((2, 4, rows, BLOCK), BF16),
                pltpu.VMEM((rows, width), BF16),
                pltpu.VMEM((rows, 2 * width), F32),
                pltpu.VMEM((rows, 3 * width), BF16),
                pltpu.VMEM((halo2, 2 * width), BF16),
                pltpu.VMEM((2, halo2, 2 * width), BF16),
                pltpu.VMEM((rows, width), BF16),
                pltpu.VMEM((rows, width), BF16),
                pltpu.VMEM((16, width), F32),
                pltpu.VMEM((8, rows), F32),
                pltpu.VMEM((stages, 16, width), F32),
                pltpu.SemaphoreType.DMA((4,)),
                pltpu.SemaphoreType.DMA((8, 2)),
                pltpu.SemaphoreType.DMA((8, 2)),
                pltpu.SemaphoreType.DMA((stages, max(used))),
                pltpu.SemaphoreType.DMA((stages, max(used))),
                pltpu.SemaphoreType.DMA((stages - 1, max(sems))),
                pltpu.SemaphoreType.DMA((stages - 1, max(sems))),
                pltpu.SemaphoreType.DMA((stages,)),
                pltpu.SemaphoreType.DMA((stages,)),
                pltpu.SemaphoreType.REGULAR((stages,)),
                *(pltpu.VMEM((count, *shape), BF16) for count, shape in zip(used, boxes)),
            ],
            compiler_params=pltpu.CompilerParams(
                collective_id=0, has_side_effects=True, vmem_limit_bytes=49 * 2**20
            ),
        )(noise.reshape(1, 1), sizes.reshape(1, 1), send.reshape(1, -1), nbr, cond_w, freq, nodes, qkv, out, up, down, cot)
        held = [pltpu.with_memory_space_constraint(v, pltpu.VMEM) for v in held]
        result, igrad, cond_grad, *grads = pl.pallas_call(
            widen,
            out_shape=(
                jax.ShapeDtypeStruct((1, rows, width), BF16),
                jax.ShapeDtypeStruct((1, rows, width), F32),
                jax.ShapeDtypeStruct(cond_w.shape, F32),
                *(jax.ShapeDtypeStruct(v.shape, F32) for v in (qkv, out, up, down)),
            ),
            in_specs=[vmem] * 4,
            out_specs=(hbm,) * 7,
            scratch_shapes=[
                pltpu.VMEM((8, BLOCK, BLOCK), F32),
                pltpu.SemaphoreType.DMA((8,)),
                pltpu.SemaphoreType.DMA((3,)),
            ],
            compiler_params=pltpu.CompilerParams(vmem_limit_bytes=32 * 2**20),
        )(*held)
        return (result, igrad, *grads, cond_grad)

    placed = (
        P("noise", "patch", None),
        P("noise"),
        P("patch"),
        P("patch"),
        P(None, "patch"),
        P(),
        P(),
        P(),
        P(),
        P(),
        P("noise", "patch", None),
    )
    return jax.shard_map(
        shards,
        mesh=mesh,
        in_specs=placed,
        out_specs=(P("noise", "patch", None), P("noise", "patch", None), P(), P(), P(), P(), P()),
        check_vma=False,
    )
```

```python
import functools

import jax
import jax.numpy as jnp
import numpy as np
from jax import lax
from jax.experimental import pallas as pl
from jax.experimental.pallas import tpu as pltpu
from jax.sharding import PartitionSpec as P

HEADS = 4
COND = 32
SLOTS = 16
EPSILON = 1e-05
LOG2E = 1.4426950408889634
MESH = pl.DeviceIdType.MESH
F32 = jnp.float32
BF16 = jnp.bfloat16
BLOCK = 512


def steps(row, cols, side, order, position):
    size, out = BLOCK // 2, []
    for d in order:
        first, width = cols
        bit = position[d]
        if d == order[-1]:
            out.append((row, row, size, cols, cols, 0, (side * width, width), d))
        elif size >= 32:
            size //= 2
            keep, send = row + bit * size, row + (1 - bit) * size
            out.append((keep, send, size, cols, cols, 0, (side * width, width), d))
            row = keep
        else:
            width //= 2
            cols, sent = (first + bit * width, width), (first + (1 - bit) * width, width)
            out.append((row, row, size, cols, sent, 0, (side * width, width), d))
    return out


def exchanges(position, line_bits, flow):
    half, line = BLOCK // 2, list(range(line_bits))
    orders = {
        0: (["x", "y", *line], ["y", "x", *line]),
        1: (["x", *line, "y"], ["y", *line, "x"]),
        2: (["x", *line, "y"], ["y", "x", *line]),
        3: (["x", "y", *line], ["y", *line, "x"]),
        4: ([*line, "x", "y"], [*line, "y", "x"]),
    }[flow]
    row, other = position["core"] * half, (1 - position["core"]) * half
    cols = (0, BLOCK)
    out = [[(row, other, half, cols, cols, 0, cols, "core")]]
    left = steps(row, (0, half), 0, orders[0], position)
    right = steps(row, (half, half), 1, orders[1], position)
    return out + [list(both) for both in zip(left, right)]


FLOWS = (0, 0, 0, 0, 0, 4, 0, 0, 0, 0, 0, 0, 0, 4, 0, 0, 0, 0, 4, 0, 0, 4, 0, 0)


def plans_for(position, line_bits):
    made = {f: exchanges(position, line_bits, f) for f in (set(FLOWS) if line_bits == 2 else {0})}
    return [made[FLOWS[n] if line_bits == 2 else 0] for n in range(24)]


def nowhere(line_bits):
    return dict.fromkeys(["core", "x", "y", *range(line_bits)], 0)


MADE = {
    **{f"down{f}": f for f in range(4)},
    **{f"up{f}": 4 + f for f in range(4)},
    **{"out": 8, "query": 9, "key": 10, "value": 11},
}
LAYER_PIECES = (
    (
        "down0", "feed0", "down1", "feed1", "down2", "feed2", "down3", "feed3", "norm2", "up0", "attended",
        "head0", "up1", "head1", "head2", "halo0", "up2", "head3", "halo1", "up3", "query", "out", "table",
        "key", "value", "norm1",
    ),
    (
        "down0", "feed0", "down1", "up0", "down2", "down3", "feed1", "feed2", "feed3", "norm2", "up1",
        "attended", "up3", "head0", "head1", "up2", "halo0", "head2", "head3", "halo1", "out", "query",
        "table", "key", "value", "norm1",
    ),
)

REDUCE_LAGS = (
    (1, 3, 3, 3, 3),
    (1, 3, 3, 3, 3),
    (1, 3, 3, 3, 3),
    (1, 3, 2, 3, 4),
    (1, 3, 3, 2, 4),
)
GATHER_LAGS = (
    (3, 4, 9, 4),
    (3, 4, 8, 5),
    (3, 4, 8, 5),
    (3, 4, 8, 5),
    (5, 3, 7, 11),
)
GATHER_WAIT = (1, 1, 1, 1, 1)
SUMS_LAG = 3


def schedule(line_bits, slots):
    tables = plans_for(nowhere(line_bits), line_bits)
    stages = 3 + line_bits
    sum_dirs = ["core", "x", *range(line_bits), "y"]

    def dirs_of(kind, s, n):
        if kind == "sums":
            return {sum_dirs[s]}
        return {p[7] for p in tables[n][s]}

    order, sent, seen = [], [], set()
    reduced = {}
    places = {}

    def told(since, dirs):
        return all(
            any(at > since and d in ds and key in seen for at, ds, key in sent) for d in dirs
        )

    def find_slot(kind, s, dirs):
        for slot in range(slots):
            since = places.get((kind, s, slot), -1)
            if since == -1 or (since is not None and told(since, dirs)):
                return slot
        return None

    def lag(kind, s, n):
        if kind == "sums":
            return SUMS_LAG
        lags = (REDUCE_LAGS if kind == "reduce" else GATHER_LAGS)[FLOWS[n]]
        if kind == "reduce":
            return lags[min(s, len(lags) - 1)]
        return lags[max(0, len(lags) - 1 - s)]

    flying, waiting = [], []

    def start_due(turn):
        for item in sorted(v for v in waiting if v[0] <= turn):
            _, kind, s, n = item
            dirs = dirs_of(kind, s, n)
            if kind == "gather" and not told(reduced[s, n], dirs):
                continue
            slot = 0 if kind == "sums" else find_slot(kind, s, dirs)
            if slot is None:
                continue
            waiting.remove(item)
            order.append(("send", kind, s, n, slot))
            places[kind, s, slot] = None
            sent.append((len(order), dirs, (kind, s, n)))
            flying.append((turn + lag(kind, s, n), kind, s, n, slot))

    def take_turn(turn):
        due = [v for v in flying if v[0] <= turn]
        rank = {"gather": 0, "sums": 1, "reduce": 2}
        due.sort(key=lambda v: (rank[v[1]], v[2] if v[1] == "gather" else -v[2], v[3]))
        for item in due:
            flying.remove(item)
            _, kind, s, n, slot = item
            order.append(("take", kind, s, n, slot))
            seen.add((kind, s, n))
            places[kind, s, slot] = len(order)
            if kind == "reduce":
                reduced[s, n] = len(order)
                if s + 1 < stages:
                    waiting.append((turn, kind, s + 1, n))
                else:
                    wait = GATHER_WAIT[FLOWS[n]]
                    waiting.append((turn + wait, "gather", s - 1, n))
            elif kind == "gather" and s > 0:
                waiting.append((turn, kind, s - 1, n))
            elif kind == "sums" and s + 1 < len(sum_dirs):
                waiting.append((turn, kind, s + 1, n))
            start_due(turn)
        start_due(turn)

    turn = 0
    for i in range(2):
        for name in LAYER_PIECES[i]:
            order.append(("work", name, i))
            if name in MADE:
                waiting.append((turn, "reduce", 0, i * 12 + MADE[name]))
                take_turn(turn)
                turn += 1
    waiting.append((turn, "sums", 0, 0))
    while flying or waiting:
        before = len(order)
        take_turn(turn)
        turn += 1
        if len(order) == before and not flying:
            for d in dirs_of(*waiting[0][1:]):
                order += [("send", "token", d, 0, 0), ("take", "token", d, 0, 0)]
                sent.append((len(order), {d}, ("token", len(order))))
                seen.add(("token", len(order)))
    return order


def nn(a, b):
    return lax.dot_general(a, b, (((1,), (0,)), ((), ())), preferred_element_type=F32)


def nt(a, b):
    return lax.dot_general(a, b, (((1,), (1,)), ((), ())), preferred_element_type=F32)


def tn(a, b):
    return lax.dot_general(a, b, (((0,), (0,)), ((), ())), preferred_element_type=F32)


def mega(
    patches,
    order,
    first_sem,
    noise_ref,
    sizes_ref,
    send_ref,
    nbr_ref,
    cond_w_ref,
    freq_ref,
    nodes_hbm,
    qkv_hbm,
    out_hbm,
    up_hbm,
    down_hbm,
    cot_hbm,
    result_ref,
    igrad_ref,
    cond_grad_ref,
    w,
    logc,
    sel,
    sel_t,
    cond,
    hid,
    mid,
    xh1,
    xh2,
    rs1,
    rs2,
    act1,
    act2,
    low,
    tr,
    qv,
    kv,
    prob,
    att_t,
    gate,
    slope,
    dob,
    dkv,
    dqkv,
    rim,
    rin,
    node_in,
    cot_in,
    sums,
    stat,
    fade,
    sums_in,
    load_sem,
    halo_send,
    halo_recv,
    block_send,
    block_recv,
    sum_send,
    sum_recv,
    token,
    *inbox,
):
    rows = hid.shape[0]
    table = kv.shape[1]
    halo = rim.shape[0] // 2
    my_noise = lax.axis_index("noise")
    me = lax.axis_index("patch")
    before = (my_noise, lax.rem(me + patches - 1, patches))
    after = (my_noise, lax.rem(me + 1, patches))

    def place(t, k, down, up, out, qkv):
        if k < 4:
            return down.at[t, pl.ds(k * BLOCK, BLOCK), :]
        if k < 8:
            return up.at[t, :, pl.ds((k - 4) * BLOCK, BLOCK)]
        if k < 9:
            return out.at[t]
        return qkv.at[t, :, pl.ds((k - 9) * BLOCK, BLOCK)]

    def load(t, k):
        src = place(t, k, down_hbm, up_hbm, out_hbm, qkv_hbm)
        return pltpu.make_async_copy(src, w.at[(1 - t) * 12 + k], load_sem.at[t, k // 8])

    node_copy = pltpu.make_async_copy(nodes_hbm.at[0], node_in, load_sem.at[2, 0])
    cot_copy = pltpu.make_async_copy(cot_hbm.at[0], cot_in, load_sem.at[2, 1])
    node_copy.start()
    for t in range(2):
        for k in (9, 10, 11, 8, 4, 0, 5, 1, 6, 2, 7, 3):
            load(t, k).start()
    cot_copy.start()

    core = lax.rem(me, 2)
    x = lax.rem(me // 2, 2)
    y = my_noise
    z = me // 4
    line = patches // 4
    core_peer = (my_noise, me + 1 - 2 * core)
    x_peer = (my_noise, me + 2 - 4 * x)
    y_peer = (1 - my_noise, me)

    barrier = pltpu.get_barrier_semaphore()
    greeted = [before, after, core_peer, x_peer, y_peer]
    for b in range(line.bit_length() - 1):
        bit = lax.rem(z // (1 << b), 2)
        greeted.append((my_noise, me + 4 * (1 << b) * (1 - 2 * bit)))
    for other in greeted:
        pl.semaphore_signal(barrier, inc=1, device_id=other, device_id_type=MESH)

    step_rows = 64

    def count(i, _):
        base = i * step_rows
        ids = lax.broadcasted_iota(jnp.int32, (step_rows, rows), 0) + base
        total = jnp.zeros((step_rows, rows), F32)
        for j in range(nbr_ref.shape[0]):
            total = total + jnp.where(nbr_ref[j : j + 1, :] == ids, 1.0, 0.0)
        logc[pl.ds(base, step_rows), :] = jnp.where(total > 0.0, jnp.log(total) * LOG2E, -1e30)
        return 0

    lax.fori_loop(0, table // step_rows, count, 0)
    picked = jnp.where(
        lax.broadcasted_iota(jnp.int32, (rows, 2 * halo), 0) == send_ref[...], 1.0, 0.0
    )
    sel_t[...] = picked.astype(BF16)
    sel[...] = picked.T.astype(BF16)

    def features(noise):
        phase = jnp.log(noise) * freq_ref[...]
        is_sin = lax.broadcasted_iota(jnp.int32, (COND, 128), 0) < COND // 2
        feats = jnp.where(is_sin, jnp.sin(phase), jnp.cos(phase))
        return jnp.concatenate([feats] * (hid.shape[1] // 128), axis=1)

    wide = features(jnp.broadcast_to(noise_ref[...], (COND, 128)))
    sums[8:16, :] = jnp.broadcast_to(noise_ref[...], (8, hid.shape[1]))
    for t in range(2):
        for i in range(4):
            cond[t * 4 + i] = jnp.sum(cond_w_ref[t, i].astype(F32) * wide, 0, keepdims=True)

    node_copy.wait()
    hid[...] = node_in[...].astype(F32)
    pl.semaphore_wait(barrier, len(greeted))

    head = hid.shape[1] // HEADS
    unit = LOG2E * head ** (-0.5)
    ln_rows = 64

    def norm(value_ref, t, first, normed_ref, inv_ref, out_ref):
        def body(i, _):
            at = pl.ds(i * ln_rows, ln_rows)
            value = value_ref[at, :]
            centred = value - jnp.mean(value, -1, keepdims=True)
            inv = lax.rsqrt(jnp.mean(centred * centred, -1, keepdims=True) + EPSILON)
            normed = centred * inv
            normed_ref[t, at, :] = normed
            inv_ref[t, at, :] = inv
            out_ref[t, at, :] = (
                normed * (1.0 + cond[t * 4 + first]) + cond[t * 4 + first + 1]
            ).astype(BF16)
            return 0

        lax.fori_loop(0, rows // ln_rows, body, 0, unroll=8)

    def halo_copies(stage, part, src, dst, to_before, to_after):
        cols = pl.ds(part * BLOCK, BLOCK)
        return [
            pltpu.make_async_remote_copy(
                src_ref=src.at[pl.ds(i * halo, halo), cols],
                dst_ref=dst.at[pl.ds(row, halo), cols],
                send_sem=halo_send.at[stage * 2 + part, i],
                recv_sem=halo_recv.at[stage * 2 + part, i],
                device_id=other,
                device_id_type=MESH,
            )
            for i, (row, other) in enumerate(((to_before, before), (to_after, after)))
        ]

    def forward(t, _):
        base = (1 - t) * 12
        norm(hid, t, 0, xh1, rs1, act1)
        loaded = w.at[pl.ds(base + 8, 4)]
        pltpu.make_async_copy(loaded, loaded, load_sem.at[t, 1]).wait()
        a = act1[t]
        copies = []
        for part in range(2):
            cols = pl.ds(part * BLOCK, BLOCK)
            kv[t, pl.ds(0, rows), cols] = nn(a, w[base + 10 + part]).astype(BF16)
            rim[:, cols] = nn(sel[...], kv[t, pl.ds(0, rows), cols]).astype(BF16)
            copies.append(halo_copies(t, part, rim, kv.at[t], rows + halo, rows))
            for copy in copies[part]:
                copy.start()
        qv[t] = nn(a, w[base + 9]).astype(BF16)
        own, far = pl.ds(0, rows), pl.ds(rows, table - rows)
        for h in range(HEADS):
            lanes = pl.ds(h * head, head)
            for c in range(2):
                cols = pl.ds(c * 256, 256)
                score = nt(kv[t, own, lanes], qv[t, cols, lanes]) * unit + logc[own, cols]
                top = jnp.max(score, 0, keepdims=True)
                part = jnp.exp2(score - top)
                prob[t, h, own, cols] = part.astype(BF16)
                stat[2 * h : 2 * h + 1, cols] = top
                stat[2 * h + 1 : 2 * h + 2, cols] = jnp.sum(part, 0, keepdims=True)
            mid[lanes, :] = tn(kv[t, own, pl.ds(BLOCK + h * head, head)], prob[t, h, own, :])
        for copy in copies[0]:
            copy.wait()
        for h in range(HEADS):
            lanes = pl.ds(h * head, head)
            score = nt(kv[t, far, lanes], qv[t, :, lanes]) * unit + logc[far, :]
            near_top = stat[2 * h : 2 * h + 1, :]
            top = jnp.maximum(near_top, jnp.max(score, 0, keepdims=True))
            part = jnp.exp2(score - top)
            scale = jnp.exp2(near_top - top)
            inv = 1.0 / (stat[2 * h + 1 : 2 * h + 2, :] * scale + jnp.sum(part, 0, keepdims=True))
            prob[t, h, far, :] = (part * inv).astype(BF16)
            fade[t, h : h + 1, :] = scale * inv
        for copy in copies[1]:
            copy.wait()
        for h in range(HEADS):
            lanes = pl.ds(h * head, head)
            near = mid[lanes, :] * fade[t, h : h + 1, :]
            values = kv[t, far, pl.ds(BLOCK + h * head, head)]
            att_t[t, lanes, :] = (near + tn(values, prob[t, h, far, :])).astype(BF16)
        mid[...] = hid[...] + tn(att_t[t], w[base + 8])
        norm(mid, t, 2, xh2, rs2, act2)
        loaded = w.at[pl.ds(base, 8)]
        pltpu.make_async_copy(loaded, loaded, load_sem.at[t, 0]).wait()
        for f in range(4):
            u = nn(act2[t], w[base + 4 + f])
            sig = 0.5 * jnp.tanh(0.5 * u) + 0.5
            g = u * sig
            gate[t, f] = g.astype(BF16)
            slope[t, f] = (sig + g * (1.0 - sig)).astype(BF16)
            if f == 0:
                hid[...] = mid[...] + nn(gate[t, f], w[base + f])
            else:
                hid[...] += nn(gate[t, f], w[base + f])
        return 0

    lax.fori_loop(0, 2, forward, 0)

    cot_copy.wait()

    def turn(i, _):
        at = pl.ds(i * ln_rows, ln_rows)
        ids = lax.broadcasted_iota(jnp.int32, (ln_rows, hid.shape[1]), 0) + i * ln_rows
        live = ids < sizes_ref[...]
        result_ref[0, at, :] = jnp.where(live, hid[at, :], 0.0).astype(BF16)
        start = jnp.where(live, cot_in[at, :].astype(F32), 0.0)
        hid[at, :] = start
        low[at, :] = start.astype(BF16)
        return 0

    lax.fori_loop(0, rows // ln_rows, turn, 0, unroll=8)

    def norm_back(t, first, grad_ref, normed_ref, inv_ref, add_ref, out_ref):
        def body(i, carry):
            scale_sum, shift_sum = carry
            at = pl.ds(i * ln_rows, ln_rows)
            grad = grad_ref[at, :]
            normed = normed_ref[t, at, :]
            back = grad * normed
            scale_sum = scale_sum + jnp.sum(back.reshape(-1, 8, hid.shape[1]), 0)
            shift_sum = shift_sum + jnp.sum(grad.reshape(-1, 8, hid.shape[1]), 0)
            scaled = grad * (1.0 + cond[t * 4 + first])
            one = jnp.mean(scaled, -1, keepdims=True)
            two = jnp.mean(scaled * normed, -1, keepdims=True)
            out = add_ref[at, :] + inv_ref[t, at, :] * (scaled - one - normed * two)
            out_ref[at, :] = out
            low[at, :] = out.astype(BF16)
            return scale_sum, shift_sum

        zero = jnp.zeros((8, hid.shape[1]), F32)
        scale_sum, shift_sum = lax.fori_loop(0, rows // ln_rows, body, (zero, zero), unroll=4)
        sums[pl.ds(t * 4 + first, 1), :] = jnp.sum(scale_sum, 0, keepdims=True)
        sums[pl.ds(t * 4 + first + 1, 1), :] = jnp.sum(shift_sum, 0, keepdims=True)

    bits = [lax.rem(z // (1 << b), 2) for b in range(line.bit_length() - 1)]
    stages = 3 + len(bits)
    position = {"core": core, "x": x, "y": y, **dict(enumerate(bits))}
    plans = plans_for(position, len(bits))
    peers = {"core": core_peer, "x": x_peer, "y": y_peer}
    for b, bit in enumerate(bits):
        peers[b] = (my_noise, me + 4 * (1 << b) * (1 - 2 * bit))

    def parts_of(s, n):
        return plans[n][s]

    def box(row, size, cols):
        at = pl.ds(row if isinstance(row, int) else pl.multiple_of(row, 16), size)
        first = cols[0] if isinstance(cols[0], int) else pl.multiple_of(cols[0], 128)
        return at, pl.ds(first, cols[1])

    def copy_to(d, src, dst, pair):
        pltpu.make_async_remote_copy(
            src_ref=src,
            dst_ref=dst,
            send_sem=pair[0],
            recv_sem=pair[1],
            device_id=peers[d],
            device_id_type=MESH,
        ).start()

    def pair_of(kind, s, slot):
        at = first_sem[kind, s] + slot
        return block_send.at[at], block_recv.at[at]

    def send_block(kind, s, n, slot):
        pair = pair_of(kind, s, slot)
        for keep, send, size, cols, sent_cols, at, at_cols, d in parts_of(s, n):
            if kind == "reduce":
                copy_to(
                    d, w.at[n, *box(send, size, sent_cols)], inbox[s].at[slot, *box(at, size, at_cols)], pair
                )
            else:
                own = w.at[n, *box(keep, size, cols)]
                copy_to(d, own, own, pair)

    def settle(like, pair):
        for sem in pair:
            pltpu.make_async_copy(like, like, sem).wait()

    def take_block(kind, s, n, slot):
        settle(inbox[s].at[slot if kind == "reduce" else 0], pair_of(kind, s, slot))
        if kind == "reduce":
            for keep, _, size, cols, _, at, at_cols, _ in parts_of(s, n):
                step = min(size, 64)

                def add(i, _, keep=keep, cols=cols, at=at, at_cols=at_cols, step=step):
                    mine = (n, *box(keep + i * step, step, cols))
                    got = inbox[s][slot, *box(at + i * step, step, at_cols)]
                    w[mine] = w[mine] + got
                    return 0

                lax.fori_loop(0, size // step, add, 0)

    sum_dirs = ["core", "x", *range(len(bits)), "y"]

    def sum_rows(s):
        return pl.ds(0, 8 if s + 1 < len(sum_dirs) else 16)

    def send_sums(s):
        src, dst = sums.at[sum_rows(s)], sums_in.at[s, sum_rows(s)]
        copy_to(sum_dirs[s], src, dst, (sum_send.at[s], sum_recv.at[s]))

    def take_sums(s):
        settle(sums_in.at[s, sum_rows(s)], (sum_send.at[s], sum_recv.at[s]))
        if s + 1 < len(sum_dirs):
            sums[0:8, :] = sums[0:8, :] + sums_in[s, 0:8, :]

    def pieces_of(i):
        t = 1 - i
        base = i * 12
        work = {}

        def down(f):
            slope[t, f] = (nt(low[...], w[base + f]) * slope[t, f].astype(F32)).astype(BF16)
            w[base + f] = tn(gate[t, f], low[...]).astype(BF16)

        def feed(f):
            if f == 0:
                tr[...] = act2[t].T
                mid[...] = nt(slope[t, f], w[base + 4 + f])
            else:
                mid[...] += nt(slope[t, f], w[base + 4 + f])

        def up(f):
            w[base + 4 + f] = nn(tr[...], slope[t, f]).astype(BF16)

        def attended():
            dob[...] = nt(low[...], w[base + 8]).astype(BF16)

        def head_back(h):
            lanes = pl.ds(h * head, head)
            keys = kv[t, :, lanes]
            values = kv[t, :, pl.ds(BLOCK + h * head, head)]
            near = prob[t, h, pl.ds(0, rows), :].astype(F32) * fade[t, h : h + 1, :]
            share = jnp.concatenate([near, prob[t, h, pl.ds(rows, table - rows), :].astype(F32)], 0)
            weight = share.astype(BF16)
            grad_out = dob[:, lanes]
            grad_weight = nt(values, grad_out)
            spread = share * grad_weight
            delta = jnp.sum(spread, 0, keepdims=True)
            ds = (spread - share * delta).astype(BF16)
            dv = nn(weight, grad_out)
            dk = nn(ds, qv[t, :, lanes]) * (head ** (-0.5))
            dq_t = tn(keys, ds) * (head ** (-0.5))
            dqkv[:, lanes] = dq_t.T.astype(BF16)
            dkv[:, lanes] = dk[:rows]
            dkv[:, pl.ds(BLOCK + h * head, head)] = dv[:rows]
            first = (h // 2) * BLOCK + (h % 2) * head
            rim[:, pl.ds(first, head)] = dk[rows:].astype(BF16)
            rim[:, pl.ds(first + BLOCK // 2, head)] = dv[rows:].astype(BF16)

        copies = []

        def send_halo(part):
            copies.extend(halo_copies(2 + t, part, rim, rin.at[t], halo, 0))
            for copy in copies[-2:]:
                copy.start()

        def out():
            w[base + 8] = nn(att_t[t], low[...]).astype(BF16)

        def project(k):
            lanes = pl.ds(k * BLOCK, BLOCK)
            back = nt(dqkv[:, lanes], w[base + 9 + k])
            if k == 0:
                tr[...] = act1[t].T
                hid[...] = back
            else:
                hid[...] += back
            w[base + 9 + k] = nn(tr[...], dqkv[:, lanes]).astype(BF16)

        def whole_table():
            for copy in copies:
                copy.wait()
            for part in range(2):
                back = nn(sel_t[...], rin[t, :, pl.ds(part * BLOCK, BLOCK)])
                for i in range(2):
                    half = BLOCK // 2
                    first = i * BLOCK + part * half
                    total = dkv[:, pl.ds(first, half)] + back[:, i * half : (i + 1) * half]
                    dqkv[:, pl.ds(BLOCK + first, half)] = total.astype(BF16)

        for f in range(4):
            work[f"down{f}"] = functools.partial(down, f)
            work[f"feed{f}"] = functools.partial(feed, f)
            work[f"up{f}"] = functools.partial(up, f)
            work[f"head{f}"] = functools.partial(head_back, f)
        work["norm2"] = functools.partial(norm_back, t, 2, mid, xh2, rs2, hid, mid)
        work["attended"] = attended
        work["halo0"] = functools.partial(send_halo, 0)
        work["halo1"] = functools.partial(send_halo, 1)
        work["out"] = out
        work["query"] = functools.partial(project, 0)
        work["table"] = whole_table
        work["key"] = functools.partial(project, 1)
        work["value"] = functools.partial(project, 2)
        work["norm1"] = functools.partial(
            norm_back, t, 0, hid, xh1, rs1, mid, hid if i == 0 else igrad_ref.at[0]
        )
        return work

    def cond_gradient():
        far_sums = len(sum_dirs) - 1
        other = features(jnp.concatenate([sums_in[far_sums, 8:16, 0:128]] * (COND // 8), axis=0))
        for t in range(2):
            for i in range(4):
                row = pl.ds(t * 4 + i, 1)
                cond_grad_ref[t, i] = wide * sums[row, :] + other * sums_in[far_sums, row, :]

    layers = [pieces_of(0), pieces_of(1)]
    for act, *rest in order:
        if act == "work":
            name, i = rest
            layers[i][name]()
        else:
            kind, s, n, slot = rest
            if kind == "sums":
                (send_sums if act == "send" else take_sums)(s)
                if act == "take" and s == len(sum_dirs) - 1:
                    cond_gradient()
            elif kind == "token":
                if act == "send":
                    told = token.at[s if isinstance(s, int) else len(bits) + "xyc".index(s[0])]
                    pl.semaphore_signal(told, inc=1, device_id=peers[s], device_id_type=MESH)
                else:
                    pl.semaphore_wait(told, 1)
            else:
                (send_block if act == "send" else take_block)(kind, s, n, slot)


def widen(
    result_in, igrad_in, cond_in, w, result, igrad, cond, qkv, out, up, down, stage, sems, small
):
    copies = [
        pltpu.make_async_copy(src, dst, small.at[i])
        for i, (src, dst) in enumerate(
            ((result_in, result), (igrad_in, igrad), (cond_in, cond))
        )
    ]
    for copy in copies:
        copy.start()
    slots = stage.shape[0]

    def leave(n, _):
        slot, k, t = lax.rem(n, slots), lax.rem(n, 12), 1 - n // 12

        @pl.when(n >= slots)
        def _():
            pltpu.make_async_copy(stage.at[slot], out.at[0], sems.at[slot]).wait()

        def convert(i, _):
            at = pl.ds(pl.multiple_of(i * 128, 128), 128)
            stage[slot, at, :] = w[n, at, :].astype(F32)
            return 0

        lax.fori_loop(0, BLOCK // 128, convert, 0)
        for first, last in ((0, 4), (4, 8), (8, 9), (9, 12)):

            @pl.when((k >= first) & (k < last))
            def _():
                at = pl.ds(pl.multiple_of((k - first) * BLOCK, BLOCK), BLOCK)
                dst = {
                    0: down.at[t, at, :],
                    4: up.at[t, :, at],
                    8: out.at[t],
                    9: qkv.at[t, :, at],
                }[first]
                pltpu.make_async_copy(stage.at[slot], dst, sems.at[slot]).start()

        return 0

    lax.fori_loop(0, 24, leave, 0)
    for slot in range(slots):
        pltpu.make_async_copy(stage.at[slot], out.at[0], sems.at[slot]).wait()
    for copy in copies:
        copy.wait()


def solution(mesh):
    patches = mesh.shape["patch"]

    def shards(nodes, noise, sizes, send, nbr, qkv, out, up, down, cond_w, cot):
        rows, width = nodes.shape[1:]
        halo2 = send.shape[0]
        halo = halo2 // 2
        table = rows + halo2
        freq = np.tile(2.0 ** (np.arange(COND) % (COND // 2) / 4.0), (128, 1)).T.astype(np.float32)
        vmem = pl.BlockSpec(memory_space=pltpu.VMEM)
        hbm = pl.BlockSpec(memory_space=pl.ANY)
        line_bits = (patches // 4).bit_length() - 1
        order = schedule(line_bits, SLOTS)
        stages = 3 + line_bits
        counts = {}
        for act, kind, s, *slot in order:
            if act == "send" and kind in ("reduce", "gather"):
                counts[kind, s] = max(counts.get((kind, s), 0), slot[1] + 1)
        first_sem, total = {}, 0
        for key, count in counts.items():
            first_sem[key] = total
            total += count
        boxes = [list(parts) for parts in plans_for(nowhere(line_bits), line_bits)[0]]
        boxes = [
            (sum(p[2] * p[3][1] for p in parts) // min(BLOCK, parts[0][6][1] * len(parts)), min(BLOCK, parts[0][6][1] * len(parts)))
            for parts in boxes
        ]
        held = pl.pallas_call(
            functools.partial(mega, patches, order, first_sem),
            out_shape=(
                pltpu.VMEM((1, rows, width), BF16),
                pltpu.VMEM((1, rows, width), F32),
                pltpu.VMEM(cond_w.shape, F32),
                pltpu.VMEM((24, BLOCK, BLOCK), BF16),
            ),
            in_specs=[vmem] * 6 + [hbm] * 6,
            out_specs=(vmem,) * 4,
            scratch_shapes=[
                pltpu.VMEM((table, rows), F32),
                pltpu.VMEM((halo2, rows), BF16),
                pltpu.VMEM((rows, halo2), BF16),
                pltpu.VMEM((8, 1, width), F32),
                pltpu.VMEM((rows, width), F32),
                pltpu.VMEM((rows, width), F32),
                pltpu.VMEM((2, rows, width), F32),
                pltpu.VMEM((2, rows, width), F32),
                pltpu.VMEM((2, rows, 1), F32),
                pltpu.VMEM((2, rows, 1), F32),
                pltpu.VMEM((2, rows, width), BF16),
                pltpu.VMEM((2, rows, width), BF16),
                pltpu.VMEM((rows, width), BF16),
                pltpu.VMEM((width, rows), BF16),
                pltpu.VMEM((2, rows, width), BF16),
                pltpu.VMEM((2, table, 2 * width), BF16),
                pltpu.VMEM((2, HEADS, table, rows), BF16),
                pltpu.VMEM((2, width, rows), BF16),
                pltpu.VMEM((2, 4, rows, BLOCK), BF16),
                pltpu.VMEM((2, 4, rows, BLOCK), BF16),
                pltpu.VMEM((rows, width), BF16),
                pltpu.VMEM((rows, 2 * width), F32),
                pltpu.VMEM((rows, 3 * width), BF16),
                pltpu.VMEM((halo2, 2 * width), BF16),
                pltpu.VMEM((2, halo2, 2 * width), BF16),
                pltpu.VMEM((rows, width), BF16),
                pltpu.VMEM((rows, width), BF16),
                pltpu.VMEM((16, width), F32),
                pltpu.VMEM((8, rows), F32),
                pltpu.VMEM((2, 8, rows), F32),
                pltpu.VMEM((stages, 16, width), F32),
                pltpu.SemaphoreType.DMA((3, 2)),
                pltpu.SemaphoreType.DMA((8, 2)),
                pltpu.SemaphoreType.DMA((8, 2)),
                pltpu.SemaphoreType.DMA((sum(counts.values()),)),
                pltpu.SemaphoreType.DMA((sum(counts.values()),)),
                pltpu.SemaphoreType.DMA((stages,)),
                pltpu.SemaphoreType.DMA((stages,)),
                pltpu.SemaphoreType.REGULAR((stages,)),
                *(pltpu.VMEM((count, *shape), BF16) for count, shape in zip((counts["reduce", s] for s in range(stages)), boxes)),
            ],
            compiler_params=pltpu.CompilerParams(
                collective_id=0, has_side_effects=True, vmem_limit_bytes=49 * 2**20
            ),
        )(noise.reshape(1, 1), sizes.reshape(1, 1), send.reshape(1, -1), nbr, cond_w, freq, nodes, qkv, out, up, down, cot)
        held = [pltpu.with_memory_space_constraint(v, pltpu.VMEM) for v in held]
        result, igrad, cond_grad, *grads = pl.pallas_call(
            widen,
            out_shape=(
                jax.ShapeDtypeStruct((1, rows, width), BF16),
                jax.ShapeDtypeStruct((1, rows, width), F32),
                jax.ShapeDtypeStruct(cond_w.shape, F32),
                *(jax.ShapeDtypeStruct(v.shape, F32) for v in (qkv, out, up, down)),
            ),
            in_specs=[vmem] * 4,
            out_specs=(hbm,) * 7,
            scratch_shapes=[
                pltpu.VMEM((8, BLOCK, BLOCK), F32),
                pltpu.SemaphoreType.DMA((8,)),
                pltpu.SemaphoreType.DMA((3,)),
            ],
            compiler_params=pltpu.CompilerParams(vmem_limit_bytes=32 * 2**20),
        )(*held)
        return (result, igrad, *grads, cond_grad)

    placed = (
        P("noise", "patch", None),
        P("noise"),
        P("patch"),
        P("patch"),
        P(None, "patch"),
        P(),
        P(),
        P(),
        P(),
        P(),
        P("noise", "patch", None),
    )
    return jax.shard_map(
        shards,
        mesh=mesh,
        in_specs=placed,
        out_specs=(P("noise", "patch", None), P("noise", "patch", None), P(), P(), P(), P(), P()),
        check_vma=False,
    )
```

```python
import functools

import jax
import jax.numpy as jnp
import numpy as np
from jax import lax
from jax.experimental import pallas as pl
from jax.experimental.pallas import tpu as pltpu
from jax.sharding import PartitionSpec as P

HEADS = 4
COND = 32
SLOTS = 16
EPSILON = 1e-05
LOG2E = 1.4426950408889634
MESH = pl.DeviceIdType.MESH
F32 = jnp.float32
BF16 = jnp.bfloat16
BLOCK = 512


def steps(row, cols, side, order, position):
    size, out = BLOCK // 2, []
    for d in order:
        first, width = cols
        bit = position[d]
        if d == order[-1]:
            out.append((row, row, size, cols, cols, 0, (side * width, width), d))
        elif size >= 32:
            size //= 2
            keep, send = row + bit * size, row + (1 - bit) * size
            out.append((keep, send, size, cols, cols, 0, (side * width, width), d))
            row = keep
        else:
            width //= 2
            cols, sent = (first + bit * width, width), (first + (1 - bit) * width, width)
            out.append((row, row, size, cols, sent, 0, (side * width, width), d))
    return out


def exchanges(position, line_bits, flow):
    half, line = BLOCK // 2, list(range(line_bits))
    orders = {
        0: (["x", "y", *line], ["y", "x", *line]),
        1: (["x", *line, "y"], ["y", *line, "x"]),
        2: (["x", *line, "y"], ["y", "x", *line]),
        3: (["x", "y", *line], ["y", *line, "x"]),
        4: ([*line, "x", "y"], [*line, "y", "x"]),
    }[flow]
    row, other = position["core"] * half, (1 - position["core"]) * half
    cols = (0, BLOCK)
    out = [[(row, other, half, cols, cols, 0, cols, "core")]]
    left = steps(row, (0, half), 0, orders[0], position)
    right = steps(row, (half, half), 1, orders[1], position)
    return out + [list(both) for both in zip(left, right)]


FLOWS = (0, 0, 0, 0, 0, 4, 0, 0, 0, 0, 0, 0, 0, 4, 0, 0, 0, 0, 4, 0, 0, 4, 0, 0)


def plans_for(position, line_bits):
    made = {f: exchanges(position, line_bits, f) for f in (set(FLOWS) if line_bits == 2 else {0})}
    return [made[FLOWS[n] if line_bits == 2 else 0] for n in range(24)]


def nowhere(line_bits):
    return dict.fromkeys(["core", "x", "y", *range(line_bits)], 0)


MADE = {
    **{f"down{f}": f for f in range(4)},
    **{f"up{f}": 4 + f for f in range(4)},
    **{"out": 8, "query": 9, "key": 10, "value": 11},
}
LAYER_PIECES = (
    (
        "down0", "feed0", "down1", "feed1", "down2", "feed2", "down3", "feed3", "norm2", "up0", "attended",
        "head0", "up1", "head1", "head2", "halo0", "up2", "head3", "halo1", "up3", "query", "out", "table",
        "key", "value", "norm1",
    ),
    (
        "down0", "feed0", "down1", "up0", "down2", "down3", "feed1", "feed2", "feed3", "norm2", "up1",
        "attended", "up3", "head0", "head1", "up2", "halo0", "head2", "head3", "halo1", "out", "query",
        "table", "key", "value", "norm1",
    ),
)

REDUCE_LAGS = (
    (1, 3, 3, 3, 3),
    (1, 3, 3, 3, 3),
    (1, 3, 3, 3, 3),
    (1, 3, 2, 3, 4),
    (1, 3, 3, 2, 4),
)
GATHER_LAGS = (
    (3, 4, 9, 4),
    (3, 4, 8, 5),
    (3, 4, 8, 5),
    (3, 4, 8, 5),
    (5, 3, 7, 11),
)
GATHER_WAIT = (1, 1, 1, 1, 1)
SUMS_LAG = 3


def schedule(line_bits, slots):
    tables = plans_for(nowhere(line_bits), line_bits)
    stages = 3 + line_bits
    sum_dirs = ["core", "x", *range(line_bits), "y"]

    def dirs_of(kind, s, n):
        if kind == "sums":
            return {sum_dirs[s]}
        return {p[7] for p in tables[n][s]}

    order, sent, seen = [], [], set()
    reduced = {}
    places = {}

    def told(since, dirs):
        return all(
            any(at > since and d in ds and key in seen for at, ds, key in sent) for d in dirs
        )

    def find_slot(kind, s, dirs):
        for slot in range(slots):
            since = places.get((kind, s, slot), -1)
            if since == -1 or (since is not None and told(since, dirs)):
                return slot
        return None

    def lag(kind, s, n):
        if kind == "sums":
            return SUMS_LAG
        lags = (REDUCE_LAGS if kind == "reduce" else GATHER_LAGS)[FLOWS[n]]
        if kind == "reduce":
            return lags[min(s, len(lags) - 1)]
        return lags[max(0, len(lags) - 1 - s)]

    flying, waiting = [], []

    def start_due(turn):
        for item in sorted(v for v in waiting if v[0] <= turn):
            _, kind, s, n = item
            dirs = dirs_of(kind, s, n)
            if kind == "gather" and not told(reduced[s, n], dirs):
                continue
            slot = 0 if kind == "sums" else find_slot(kind, s, dirs)
            if slot is None:
                continue
            waiting.remove(item)
            order.append(("send", kind, s, n, slot))
            places[kind, s, slot] = None
            sent.append((len(order), dirs, (kind, s, n)))
            flying.append((turn + lag(kind, s, n), kind, s, n, slot))

    def take_turn(turn):
        due = [v for v in flying if v[0] <= turn]
        rank = {"reduce": 0, "sums": 1, "gather": 2}
        due.sort(key=lambda v: (rank[v[1]], v[2] if v[1] == "gather" else -v[2], v[3]))
        for item in due:
            flying.remove(item)
            _, kind, s, n, slot = item
            order.append(("take", kind, s, n, slot))
            seen.add((kind, s, n))
            places[kind, s, slot] = len(order)
            if kind == "reduce":
                reduced[s, n] = len(order)
                if s + 1 < stages:
                    waiting.append((turn, kind, s + 1, n))
                else:
                    wait = GATHER_WAIT[FLOWS[n]]
                    waiting.append((turn + wait, "gather", s - 1, n))
            elif kind == "gather" and s > 0:
                waiting.append((turn, kind, s - 1, n))
            elif kind == "sums" and s + 1 < len(sum_dirs):
                waiting.append((turn, kind, s + 1, n))
            start_due(turn)
        start_due(turn)

    turn = 0
    for i in range(2):
        for name in LAYER_PIECES[i]:
            order.append(("work", name, i))
            if name in MADE:
                waiting.append((turn, "reduce", 0, i * 12 + MADE[name]))
                take_turn(turn)
                turn += 1
    waiting.append((turn, "sums", 0, 0))
    while flying or waiting:
        before = len(order)
        take_turn(turn)
        turn += 1
        if len(order) == before and not flying:
            for d in dirs_of(*waiting[0][1:]):
                order += [("send", "token", d, 0, 0), ("take", "token", d, 0, 0)]
                sent.append((len(order), {d}, ("token", len(order))))
                seen.add(("token", len(order)))
    return order


def nn(a, b):
    return lax.dot_general(a, b, (((1,), (0,)), ((), ())), preferred_element_type=F32)


def nt(a, b):
    return lax.dot_general(a, b, (((1,), (1,)), ((), ())), preferred_element_type=F32)


def tn(a, b):
    return lax.dot_general(a, b, (((0,), (0,)), ((), ())), preferred_element_type=F32)


def mega(
    patches,
    order,
    first_sem,
    noise_ref,
    sizes_ref,
    send_ref,
    nbr_ref,
    cond_w_ref,
    nodes_hbm,
    qkv_hbm,
    out_hbm,
    up_hbm,
    down_hbm,
    cot_hbm,
    result_ref,
    igrad_ref,
    cond_grad_ref,
    w,
    logc,
    sel,
    sel_t,
    cond,
    hid,
    mid,
    xh1,
    xh2,
    rs1,
    rs2,
    act1,
    act2,
    low,
    tr,
    qv,
    kv,
    prob,
    att_t,
    gate,
    slope,
    dob,
    dkv,
    dqkv,
    rim,
    rin,
    node_in,
    cot_in,
    sums,
    stat,
    fade,
    sums_in,
    load_sem,
    halo_send,
    halo_recv,
    block_send,
    block_recv,
    sum_send,
    sum_recv,
    token,
    *inbox,
):
    rows = hid.shape[0]
    table = kv.shape[1]
    halo = rim.shape[0] // 2
    my_noise = lax.axis_index("noise")
    me = lax.axis_index("patch")
    before = (my_noise, lax.rem(me + patches - 1, patches))
    after = (my_noise, lax.rem(me + 1, patches))

    def place(t, k, down, up, out, qkv):
        if k < 4:
            return down.at[t, pl.ds(k * BLOCK, BLOCK), :]
        if k < 8:
            return up.at[t, :, pl.ds((k - 4) * BLOCK, BLOCK)]
        if k < 9:
            return out.at[t]
        return qkv.at[t, :, pl.ds((k - 9) * BLOCK, BLOCK)]

    def load(t, k):
        src = place(t, k, down_hbm, up_hbm, out_hbm, qkv_hbm)
        return pltpu.make_async_copy(src, w.at[(1 - t) * 12 + k], load_sem.at[t, k // 8])

    node_copy = pltpu.make_async_copy(nodes_hbm.at[0], node_in, load_sem.at[2, 0])
    cot_copy = pltpu.make_async_copy(cot_hbm.at[0], cot_in, load_sem.at[2, 1])
    node_copy.start()
    for t in range(2):
        for k in (9, 10, 11, 8, 4, 0, 5, 1, 6, 2, 7, 3):
            load(t, k).start()
    cot_copy.start()

    core = lax.rem(me, 2)
    x = lax.rem(me // 2, 2)
    y = my_noise
    z = me // 4
    line = patches // 4
    core_peer = (my_noise, me + 1 - 2 * core)
    x_peer = (my_noise, me + 2 - 4 * x)
    y_peer = (1 - my_noise, me)

    barrier = pltpu.get_barrier_semaphore()
    greeted = [before, after, core_peer, x_peer, y_peer]
    for b in range(line.bit_length() - 1):
        bit = lax.rem(z // (1 << b), 2)
        greeted.append((my_noise, me + 4 * (1 << b) * (1 - 2 * bit)))
    for other in greeted:
        pl.semaphore_signal(barrier, inc=1, device_id=other, device_id_type=MESH)

    step_rows = 64

    def count(i, _):
        base = i * step_rows
        ids = lax.broadcasted_iota(jnp.int32, (step_rows, rows), 0) + base
        total = jnp.zeros((step_rows, rows), F32)
        for j in range(nbr_ref.shape[0]):
            total = total + jnp.where(nbr_ref[j : j + 1, :] == ids, 1.0, 0.0)
        logc[pl.ds(base, step_rows), :] = jnp.where(total > 0.0, jnp.log(total) * LOG2E, -1e30)
        return 0

    lax.fori_loop(0, table // step_rows, count, 0)
    picked = jnp.where(
        lax.broadcasted_iota(jnp.int32, (rows, 2 * halo), 0) == send_ref[...], 1.0, 0.0
    )
    sel_t[...] = picked.astype(BF16)
    sel[...] = picked.T.astype(BF16)

    def features(noise):
        row = lax.broadcasted_iota(jnp.int32, (COND, 128), 0)
        is_sin = row < COND // 2
        frequency = jnp.full((COND, 128), 1.0, F32)
        for i in range(1, COND // 2):
            frequency = jnp.where(row % (COND // 2) == i, np.float32(2.0 ** (i / 4)), frequency)
        phase = jnp.log(noise) * frequency
        feats = jnp.where(is_sin, jnp.sin(phase), jnp.cos(phase))
        return jnp.concatenate([feats] * (hid.shape[1] // 128), axis=1)

    wide = features(jnp.broadcast_to(noise_ref[...], (COND, 128)))
    sums[8:16, :] = jnp.broadcast_to(noise_ref[...], (8, hid.shape[1]))
    for t in range(2):
        for i in range(4):
            cond[t * 4 + i] = jnp.sum(cond_w_ref[t, i].astype(F32) * wide, 0, keepdims=True)

    node_copy.wait()
    hid[...] = node_in[...].astype(F32)
    pl.semaphore_wait(barrier, len(greeted))

    head = hid.shape[1] // HEADS
    unit = LOG2E * head ** (-0.5)
    ln_rows = 64

    def norm(value_ref, t, first, normed_ref, inv_ref, out_ref):
        def body(i, _):
            at = pl.ds(i * ln_rows, ln_rows)
            value = value_ref[at, :]
            centred = value - jnp.mean(value, -1, keepdims=True)
            inv = lax.rsqrt(jnp.mean(centred * centred, -1, keepdims=True) + EPSILON)
            normed = centred * inv
            normed_ref[t, at, :] = normed
            inv_ref[t, at, :] = inv
            out_ref[t, at, :] = (
                normed * (1.0 + cond[t * 4 + first]) + cond[t * 4 + first + 1]
            ).astype(BF16)
            return 0

        lax.fori_loop(0, rows // ln_rows, body, 0, unroll=8)

    def halo_copies(stage, part, src, dst, to_before, to_after):
        cols = pl.ds(part * BLOCK, BLOCK)
        return [
            pltpu.make_async_remote_copy(
                src_ref=src.at[pl.ds(i * halo, halo), cols],
                dst_ref=dst.at[pl.ds(row, halo), cols],
                send_sem=halo_send.at[stage * 2 + part, i],
                recv_sem=halo_recv.at[stage * 2 + part, i],
                device_id=other,
                device_id_type=MESH,
            )
            for i, (row, other) in enumerate(((to_before, before), (to_after, after)))
        ]

    def forward(t, _):
        base = (1 - t) * 12
        norm(hid, t, 0, xh1, rs1, act1)
        loaded = w.at[pl.ds(base + 8, 4)]
        pltpu.make_async_copy(loaded, loaded, load_sem.at[t, 1]).wait()
        a = act1[t]
        copies = []
        for part in range(2):
            cols = pl.ds(part * BLOCK, BLOCK)
            kv[t, pl.ds(0, rows), cols] = nn(a, w[base + 10 + part]).astype(BF16)
            rim[:, cols] = nn(sel[...], kv[t, pl.ds(0, rows), cols]).astype(BF16)
            copies.append(halo_copies(t, part, rim, kv.at[t], rows + halo, rows))
            for copy in copies[part]:
                copy.start()
        qv[t] = nn(a, w[base + 9]).astype(BF16)
        own, far = pl.ds(0, rows), pl.ds(rows, table - rows)
        for h in range(HEADS):
            lanes = pl.ds(h * head, head)
            for c in range(2):
                cols = pl.ds(c * 256, 256)
                score = nt(kv[t, own, lanes], qv[t, cols, lanes]) * unit + logc[own, cols]
                top = jnp.max(score, 0, keepdims=True)
                part = jnp.exp2(score - top)
                prob[t, h, own, cols] = part.astype(BF16)
                stat[2 * h : 2 * h + 1, cols] = top
                stat[2 * h + 1 : 2 * h + 2, cols] = jnp.sum(part, 0, keepdims=True)
            mid[lanes, :] = tn(kv[t, own, pl.ds(BLOCK + h * head, head)], prob[t, h, own, :])
        for copy in copies[0]:
            copy.wait()
        for h in range(HEADS):
            lanes = pl.ds(h * head, head)
            score = nt(kv[t, far, lanes], qv[t, :, lanes]) * unit + logc[far, :]
            near_top = stat[2 * h : 2 * h + 1, :]
            top = jnp.maximum(near_top, jnp.max(score, 0, keepdims=True))
            part = jnp.exp2(score - top)
            scale = jnp.exp2(near_top - top)
            inv = 1.0 / (stat[2 * h + 1 : 2 * h + 2, :] * scale + jnp.sum(part, 0, keepdims=True))
            prob[t, h, far, :] = (part * inv).astype(BF16)
            fade[t, h : h + 1, :] = scale * inv
        for copy in copies[1]:
            copy.wait()
        for h in range(HEADS):
            lanes = pl.ds(h * head, head)
            near = mid[lanes, :] * fade[t, h : h + 1, :]
            values = kv[t, far, pl.ds(BLOCK + h * head, head)]
            att_t[t, lanes, :] = (near + tn(values, prob[t, h, far, :])).astype(BF16)
        mid[...] = hid[...] + tn(att_t[t], w[base + 8])
        norm(mid, t, 2, xh2, rs2, act2)
        loaded = w.at[pl.ds(base, 8)]
        pltpu.make_async_copy(loaded, loaded, load_sem.at[t, 0]).wait()
        for f in range(4):
            u = nn(act2[t], w[base + 4 + f])
            sig = 0.5 * jnp.tanh(0.5 * u) + 0.5
            g = u * sig
            gate[t, f] = g.astype(BF16)
            slope[t, f] = (sig + g * (1.0 - sig)).astype(BF16)
            if f == 0:
                hid[...] = mid[...] + nn(gate[t, f], w[base + f])
            else:
                hid[...] += nn(gate[t, f], w[base + f])
        return 0

    lax.fori_loop(0, 2, forward, 0)

    cot_copy.wait()

    def turn(i, _):
        at = pl.ds(i * ln_rows, ln_rows)
        ids = lax.broadcasted_iota(jnp.int32, (ln_rows, hid.shape[1]), 0) + i * ln_rows
        live = ids < sizes_ref[...]
        result_ref[0, at, :] = jnp.where(live, hid[at, :], 0.0).astype(BF16)
        start = jnp.where(live, cot_in[at, :].astype(F32), 0.0)
        hid[at, :] = start
        low[at, :] = start.astype(BF16)
        return 0

    lax.fori_loop(0, rows // ln_rows, turn, 0, unroll=8)

    def norm_back(t, first, grad_ref, normed_ref, inv_ref, add_ref, out_ref):
        def body(i, carry):
            scale_sum, shift_sum = carry
            at = pl.ds(i * ln_rows, ln_rows)
            grad = grad_ref[at, :]
            normed = normed_ref[t, at, :]
            back = grad * normed
            scale_sum = scale_sum + jnp.sum(back.reshape(-1, 8, hid.shape[1]), 0)
            shift_sum = shift_sum + jnp.sum(grad.reshape(-1, 8, hid.shape[1]), 0)
            scaled = grad * (1.0 + cond[t * 4 + first])
            one = jnp.mean(scaled, -1, keepdims=True)
            two = jnp.mean(scaled * normed, -1, keepdims=True)
            out = add_ref[at, :] + inv_ref[t, at, :] * (scaled - one - normed * two)
            out_ref[at, :] = out
            low[at, :] = out.astype(BF16)
            return scale_sum, shift_sum

        zero = jnp.zeros((8, hid.shape[1]), F32)
        scale_sum, shift_sum = lax.fori_loop(0, rows // ln_rows, body, (zero, zero), unroll=4)
        sums[pl.ds(t * 4 + first, 1), :] = jnp.sum(scale_sum, 0, keepdims=True)
        sums[pl.ds(t * 4 + first + 1, 1), :] = jnp.sum(shift_sum, 0, keepdims=True)

    bits = [lax.rem(z // (1 << b), 2) for b in range(line.bit_length() - 1)]
    stages = 3 + len(bits)
    position = {"core": core, "x": x, "y": y, **dict(enumerate(bits))}
    plans = plans_for(position, len(bits))
    peers = {"core": core_peer, "x": x_peer, "y": y_peer}
    for b, bit in enumerate(bits):
        peers[b] = (my_noise, me + 4 * (1 << b) * (1 - 2 * bit))

    def parts_of(s, n):
        return plans[n][s]

    def box(row, size, cols):
        at = pl.ds(row if isinstance(row, int) else pl.multiple_of(row, 16), size)
        first = cols[0] if isinstance(cols[0], int) else pl.multiple_of(cols[0], 128)
        return at, pl.ds(first, cols[1])

    def copy_to(d, src, dst, pair):
        pltpu.make_async_remote_copy(
            src_ref=src,
            dst_ref=dst,
            send_sem=pair[0],
            recv_sem=pair[1],
            device_id=peers[d],
            device_id_type=MESH,
        ).start()

    def pair_of(kind, s, slot):
        at = first_sem[kind, s] + slot
        return block_send.at[at], block_recv.at[at]

    def send_block(kind, s, n, slot):
        pair = pair_of(kind, s, slot)
        for keep, send, size, cols, sent_cols, at, at_cols, d in parts_of(s, n):
            if kind == "reduce":
                copy_to(
                    d, w.at[n, *box(send, size, sent_cols)], inbox[s].at[slot, *box(at, size, at_cols)], pair
                )
            else:
                own = w.at[n, *box(keep, size, cols)]
                copy_to(d, own, own, pair)

    def settle(like, pair):
        for sem in pair:
            pltpu.make_async_copy(like, like, sem).wait()

    def take_block(kind, s, n, slot):
        settle(inbox[s].at[slot if kind == "reduce" else 0], pair_of(kind, s, slot))
        if kind == "reduce":
            for keep, _, size, cols, _, at, at_cols, _ in parts_of(s, n):
                step = min(size, 64)

                def add(i, _, keep=keep, cols=cols, at=at, at_cols=at_cols, step=step):
                    mine = (n, *box(keep + i * step, step, cols))
                    got = inbox[s][slot, *box(at + i * step, step, at_cols)]
                    w[mine] = w[mine] + got
                    return 0

                lax.fori_loop(0, size // step, add, 0)

    sum_dirs = ["core", "x", *range(len(bits)), "y"]

    def sum_rows(s):
        return pl.ds(0, 8 if s + 1 < len(sum_dirs) else 16)

    def send_sums(s):
        src, dst = sums.at[sum_rows(s)], sums_in.at[s, sum_rows(s)]
        copy_to(sum_dirs[s], src, dst, (sum_send.at[s], sum_recv.at[s]))

    def take_sums(s):
        settle(sums_in.at[s, sum_rows(s)], (sum_send.at[s], sum_recv.at[s]))
        if s + 1 < len(sum_dirs):
            sums[0:8, :] = sums[0:8, :] + sums_in[s, 0:8, :]

    def pieces_of(i):
        t = 1 - i
        base = i * 12
        work = {}

        def down(f):
            slope[t, f] = (nt(low[...], w[base + f]) * slope[t, f].astype(F32)).astype(BF16)
            w[base + f] = tn(gate[t, f], low[...]).astype(BF16)

        def feed(f):
            if f == 0:
                tr[...] = act2[t].T
                mid[...] = nt(slope[t, f], w[base + 4 + f])
            else:
                mid[...] += nt(slope[t, f], w[base + 4 + f])

        def up(f):
            w[base + 4 + f] = nn(tr[...], slope[t, f]).astype(BF16)

        def attended():
            dob[...] = nt(low[...], w[base + 8]).astype(BF16)

        def head_back(h):
            lanes = pl.ds(h * head, head)
            keys = kv[t, :, lanes]
            values = kv[t, :, pl.ds(BLOCK + h * head, head)]
            near = prob[t, h, pl.ds(0, rows), :].astype(F32) * fade[t, h : h + 1, :]
            share = jnp.concatenate([near, prob[t, h, pl.ds(rows, table - rows), :].astype(F32)], 0)
            weight = share.astype(BF16)
            grad_out = dob[:, lanes]
            grad_weight = nt(values, grad_out)
            spread = share * grad_weight
            delta = jnp.sum(spread, 0, keepdims=True)
            ds = (spread - share * delta).astype(BF16)
            dv = nn(weight, grad_out)
            dk = nn(ds, qv[t, :, lanes]) * (head ** (-0.5))
            dq_t = tn(keys, ds) * (head ** (-0.5))
            dqkv[:, lanes] = dq_t.T.astype(BF16)
            dkv[:, lanes] = dk[:rows]
            dkv[:, pl.ds(BLOCK + h * head, head)] = dv[:rows]
            first = (h // 2) * BLOCK + (h % 2) * head
            rim[:, pl.ds(first, head)] = dk[rows:].astype(BF16)
            rim[:, pl.ds(first + BLOCK // 2, head)] = dv[rows:].astype(BF16)

        copies = []

        def send_halo(part):
            copies.extend(halo_copies(2 + t, part, rim, rin.at[t], halo, 0))
            for copy in copies[-2:]:
                copy.start()

        def out():
            w[base + 8] = nn(att_t[t], low[...]).astype(BF16)

        def project(k):
            lanes = pl.ds(k * BLOCK, BLOCK)
            back = nt(dqkv[:, lanes], w[base + 9 + k])
            if k == 0:
                tr[...] = act1[t].T
                hid[...] = back
            else:
                hid[...] += back
            w[base + 9 + k] = nn(tr[...], dqkv[:, lanes]).astype(BF16)

        def whole_table():
            for copy in copies:
                copy.wait()
            for part in range(2):
                back = nn(sel_t[...], rin[t, :, pl.ds(part * BLOCK, BLOCK)])
                for i in range(2):
                    half = BLOCK // 2
                    first = i * BLOCK + part * half
                    total = dkv[:, pl.ds(first, half)] + back[:, i * half : (i + 1) * half]
                    dqkv[:, pl.ds(BLOCK + first, half)] = total.astype(BF16)

        for f in range(4):
            work[f"down{f}"] = functools.partial(down, f)
            work[f"feed{f}"] = functools.partial(feed, f)
            work[f"up{f}"] = functools.partial(up, f)
            work[f"head{f}"] = functools.partial(head_back, f)
        work["norm2"] = functools.partial(norm_back, t, 2, mid, xh2, rs2, hid, mid)
        work["attended"] = attended
        work["halo0"] = functools.partial(send_halo, 0)
        work["halo1"] = functools.partial(send_halo, 1)
        work["out"] = out
        work["query"] = functools.partial(project, 0)
        work["table"] = whole_table
        work["key"] = functools.partial(project, 1)
        work["value"] = functools.partial(project, 2)
        work["norm1"] = functools.partial(
            norm_back, t, 0, hid, xh1, rs1, mid, hid if i == 0 else igrad_ref.at[0]
        )
        return work

    def cond_gradient():
        far_sums = len(sum_dirs) - 1
        other = features(jnp.concatenate([sums_in[far_sums, 8:16, 0:128]] * (COND // 8), axis=0))
        for t in range(2):
            for i in range(4):
                row = pl.ds(t * 4 + i, 1)
                cond_grad_ref[t, i] = wide * sums[row, :] + other * sums_in[far_sums, row, :]

    layers = [pieces_of(0), pieces_of(1)]
    for act, *rest in order:
        if act == "work":
            name, i = rest
            layers[i][name]()
        else:
            kind, s, n, slot = rest
            if kind == "sums":
                (send_sums if act == "send" else take_sums)(s)
                if act == "take" and s == len(sum_dirs) - 1:
                    cond_gradient()
            elif kind == "token":
                if act == "send":
                    told = token.at[s if isinstance(s, int) else len(bits) + "xyc".index(s[0])]
                    pl.semaphore_signal(told, inc=1, device_id=peers[s], device_id_type=MESH)
                else:
                    pl.semaphore_wait(told, 1)
            else:
                (send_block if act == "send" else take_block)(kind, s, n, slot)


def widen(
    result_in, igrad_in, cond_in, w, result, igrad, cond, qkv, out, up, down, stage, sems, small
):
    copies = [
        pltpu.make_async_copy(src, dst, small.at[i])
        for i, (src, dst) in enumerate(
            ((result_in, result), (igrad_in, igrad), (cond_in, cond))
        )
    ]
    for copy in copies:
        copy.start()
    slots = stage.shape[0]

    def leave(n, _):
        slot, k, t = lax.rem(n, slots), lax.rem(n, 12), 1 - n // 12

        @pl.when(n >= slots)
        def _():
            pltpu.make_async_copy(stage.at[slot], out.at[0], sems.at[slot]).wait()

        def convert(i, _):
            at = pl.ds(pl.multiple_of(i * 128, 128), 128)
            stage[slot, at, :] = w[n, at, :].astype(F32)
            return 0

        lax.fori_loop(0, BLOCK // 128, convert, 0, unroll=4)
        for first, last in ((0, 4), (4, 8), (8, 9), (9, 12)):

            @pl.when((k >= first) & (k < last))
            def _():
                at = pl.ds(pl.multiple_of((k - first) * BLOCK, BLOCK), BLOCK)
                dst = {
                    0: down.at[t, at, :],
                    4: up.at[t, :, at],
                    8: out.at[t],
                    9: qkv.at[t, :, at],
                }[first]
                pltpu.make_async_copy(stage.at[slot], dst, sems.at[slot]).start()

        return 0

    lax.fori_loop(0, 24, leave, 0)
    for slot in range(slots):
        pltpu.make_async_copy(stage.at[slot], out.at[0], sems.at[slot]).wait()
    for copy in copies:
        copy.wait()


def solution(mesh):
    patches = mesh.shape["patch"]

    def shards(nodes, noise, sizes, send, nbr, qkv, out, up, down, cond_w, cot):
        rows, width = nodes.shape[1:]
        halo2 = send.shape[0]
        halo = halo2 // 2
        table = rows + halo2
        vmem = pl.BlockSpec(memory_space=pltpu.VMEM)
        hbm = pl.BlockSpec(memory_space=pl.ANY)
        line_bits = (patches // 4).bit_length() - 1
        order = schedule(line_bits, SLOTS)
        stages = 3 + line_bits
        counts = {}
        for act, kind, s, *slot in order:
            if act == "send" and kind in ("reduce", "gather"):
                counts[kind, s] = max(counts.get((kind, s), 0), slot[1] + 1)
        first_sem, total = {}, 0
        for key, count in counts.items():
            first_sem[key] = total
            total += count
        boxes = [list(parts) for parts in plans_for(nowhere(line_bits), line_bits)[0]]
        boxes = [
            (sum(p[2] * p[3][1] for p in parts) // min(BLOCK, parts[0][6][1] * len(parts)), min(BLOCK, parts[0][6][1] * len(parts)))
            for parts in boxes
        ]
        held = pl.pallas_call(
            functools.partial(mega, patches, order, first_sem),
            out_shape=(
                pltpu.VMEM((1, rows, width), BF16),
                pltpu.VMEM((1, rows, width), F32),
                pltpu.VMEM(cond_w.shape, F32),
                pltpu.VMEM((24, BLOCK, BLOCK), BF16),
            ),
            in_specs=[vmem] * 5 + [hbm] * 6,
            out_specs=(vmem,) * 4,
            scratch_shapes=[
                pltpu.VMEM((table, rows), F32),
                pltpu.VMEM((halo2, rows), BF16),
                pltpu.VMEM((rows, halo2), BF16),
                pltpu.VMEM((8, 1, width), F32),
                pltpu.VMEM((rows, width), F32),
                pltpu.VMEM((rows, width), F32),
                pltpu.VMEM((2, rows, width), F32),
                pltpu.VMEM((2, rows, width), F32),
                pltpu.VMEM((2, rows, 1), F32),
                pltpu.VMEM((2, rows, 1), F32),
                pltpu.VMEM((2, rows, width), BF16),
                pltpu.VMEM((2, rows, width), BF16),
                pltpu.VMEM((rows, width), BF16),
                pltpu.VMEM((width, rows), BF16),
                pltpu.VMEM((2, rows, width), BF16),
                pltpu.VMEM((2, table, 2 * width), BF16),
                pltpu.VMEM((2, HEADS, table, rows), BF16),
                pltpu.VMEM((2, width, rows), BF16),
                pltpu.VMEM((2, 4, rows, BLOCK), BF16),
                pltpu.VMEM((2, 4, rows, BLOCK), BF16),
                pltpu.VMEM((rows, width), BF16),
                pltpu.VMEM((rows, 2 * width), F32),
                pltpu.VMEM((rows, 3 * width), BF16),
                pltpu.VMEM((halo2, 2 * width), BF16),
                pltpu.VMEM((2, halo2, 2 * width), BF16),
                pltpu.VMEM((rows, width), BF16),
                pltpu.VMEM((rows, width), BF16),
                pltpu.VMEM((16, width), F32),
                pltpu.VMEM((8, rows), F32),
                pltpu.VMEM((2, 8, rows), F32),
                pltpu.VMEM((stages, 16, width), F32),
                pltpu.SemaphoreType.DMA((3, 2)),
                pltpu.SemaphoreType.DMA((8, 2)),
                pltpu.SemaphoreType.DMA((8, 2)),
                pltpu.SemaphoreType.DMA((sum(counts.values()),)),
                pltpu.SemaphoreType.DMA((sum(counts.values()),)),
                pltpu.SemaphoreType.DMA((stages,)),
                pltpu.SemaphoreType.DMA((stages,)),
                pltpu.SemaphoreType.REGULAR((stages,)),
                *(pltpu.VMEM((count, *shape), BF16) for count, shape in zip((counts["reduce", s] for s in range(stages)), boxes)),
            ],
            compiler_params=pltpu.CompilerParams(
                collective_id=0, has_side_effects=True, vmem_limit_bytes=49 * 2**20
            ),
        )(noise.reshape(1, 1), sizes.reshape(1, 1), send.reshape(1, -1), nbr, cond_w, nodes, qkv, out, up, down, cot)
        held = [pltpu.with_memory_space_constraint(v, pltpu.VMEM) for v in held]
        result, igrad, cond_grad, *grads = pl.pallas_call(
            widen,
            out_shape=(
                jax.ShapeDtypeStruct((1, rows, width), BF16),
                jax.ShapeDtypeStruct((1, rows, width), F32),
                jax.ShapeDtypeStruct(cond_w.shape, F32),
                *(jax.ShapeDtypeStruct(v.shape, F32) for v in (qkv, out, up, down)),
            ),
            in_specs=[vmem] * 4,
            out_specs=(hbm,) * 7,
            scratch_shapes=[
                pltpu.VMEM((12, BLOCK, BLOCK), F32),
                pltpu.SemaphoreType.DMA((12,)),
                pltpu.SemaphoreType.DMA((3,)),
            ],
            compiler_params=pltpu.CompilerParams(vmem_limit_bytes=32 * 2**20),
        )(*held)
        return (result, igrad, *grads, cond_grad)

    placed = (
        P("noise", "patch", None),
        P("noise"),
        P("patch"),
        P("patch"),
        P(None, "patch"),
        P(),
        P(),
        P(),
        P(),
        P(),
        P("noise", "patch", None),
    )
    return jax.shard_map(
        shards,
        mesh=mesh,
        in_specs=placed,
        out_specs=(P("noise", "patch", None), P("noise", "patch", None), P(), P(), P(), P(), P()),
        check_vma=False,
    )
```
